256 devices in a mesh: dp: 32 (over z, x_hi, core), worker: 8 (over y, x_lo).
Axes of the slice: x: 4 (x_hi: 2, x_lo: 2; x = x_hi * 2 + x_lo), y: 4, z: 8, core: 2. Of those that a mesh axis runs over, the one named last changes fastest.
Arguments:
- acts: bfloat16 [32768, 4096], P('dp', 'worker'), may hold values from -6 to 6
- cotan: bfloat16 [32768, 4096], P('dp', 'worker'), may hold values from -0.15625 to 0.15625
- block_ids: int32 [64], P('dp'), may hold values from 0 to 7
- basis_in: bfloat16 [8, 512, 512], P('worker'), may hold values from -0.25 to 0.25
- basis_out: bfloat16 [8, 512, 512], replicated, may hold values from -0.25 to 0.25
- act_factor: float32 [8, 512, 512], P('worker'), may hold values from -0.0009375 to 1, as said below
- grad_factor: float32 [8, 512, 512], P('worker'), may hold values from -0.0009375 to 1, as said below
Outputs:
- precond: bfloat16 [4096, 4096], P('dp', 'worker')
- act_new: float32 [8, 512, 512], P('worker')
- grad_new: float32 [8, 512, 512], P('worker')
The draws below stay inside these ranges and needn't reach their ends.
Inputs may be any that keep to these rules, and one draw needn't show every extreme that they name: `act_factor`: each block is symmetric, and each diagonal entry exceeds the sum of magnitudes of the other entries of its row. `grad_factor`: each block is symmetric, and each diagonal entry exceeds the sum of magnitudes of the other entries of its row.
All inputs are finite; a program needn't handle non-finite values.
Results may differ from the reference program's by a relative error of at most 0.025.
Values may be sent and summed in bfloat16 or wider, within the bound.
A program may use at most 64 MiB of HBM per device.

```python
import jax
import jax.numpy as jnp
from jax import lax

D = 4096
FB = 512
NB = 8
BLK = 128
POOL_BLK = 8
SAMP_BLK = 2
TOKENS = 32768
SAMPLES = 8192
N_DP = 32


def dominant_blocks(key):
    diag_key, outside_key = jax.random.split(key)
    diagonal = jax.random.uniform(diag_key, (NB, FB), jnp.float32, 0.5, 1.0)
    outside = jax.random.uniform(outside_key, (NB, FB, FB), jnp.float32, -1.0, 1.0)
    outside = (outside + jnp.swapaxes(outside, 1, 2)) * (0.24 / FB)
    identity = jnp.eye(FB, dtype=jnp.float32)
    return outside * (1.0 - identity) + identity * diagonal[:, :, None]


def draw_act_factor(key, part):
    key = jax.random.fold_in(key, 11)
    return dominant_blocks(key)


def draw_grad_factor(key, part):
    key = jax.random.fold_in(key, 23)
    return dominant_blocks(key)


def with_ends(values, rng, low, top_value):
    longest = values.shape.index(max(values.shape))
    spots = []
    for shift in (0, 1):
        where = [jax.random.randint(jax.random.fold_in(rng, axis), (), 0, length) for axis, length in enumerate(values.shape)]
        where[longest] = (where[longest] + shift) % values.shape[longest]
        spots.append(tuple(where))
    return values.at[spots[0]].set(low).at[spots[1]].set(top_value)


def spiked(result, rng, source, target, shards_of, factor):
    def block_of(position):
        return (jnp.arange(result.shape[position]) // (result.shape[position] // shards_of)).reshape((-1,) + (1,) * (result.ndim - 1 - position))

    one_side = jax.random.permutation(rng, shards_of)[block_of(target)]
    far = (block_of(target) + shards_of // 2) % shards_of
    return jnp.where((block_of(source) == one_side) | (block_of(source) == far), factor * result, result)


def block_scale(rng, extent, pieces, smallest, high):
    loudness, own = 1.0, jax.random.fold_in(rng, 6)
    for position, shards_of in pieces:
        steps = jnp.exp(jax.random.uniform(jax.random.fold_in(own, position), (shards_of,), jnp.float32, smallest / len(pieces), high / len(pieces)))
        loudness = loudness * jnp.repeat(steps, extent[position] // shards_of).reshape([-1 if axis == position else 1 for axis in range(len(extent))])
    return loudness


def gaussian(key, extent, deviation, bound, shards=(), kind=jnp.bfloat16):
    array = deviation * jax.random.normal(key, extent, jnp.float32)
    if shards:
        array = array * block_scale(key, extent, shards, -0.22, 0.18)
    return jnp.clip(array, -bound, bound).astype(kind)


def heavy_noise(own_key, dims, spread, bound, shards, heavy, kind=jnp.bfloat16):
    result = spread * jax.random.normal(own_key, dims, jnp.float32)
    if shards:
        result = result * block_scale(own_key, dims, shards, -0.22, 0.18)
    return jnp.clip(spiked(result, jax.random.fold_in(own_key, 3), *heavy), -bound, bound).astype(kind)


def setup_inputs(seed: int = 0) -> dict:
    arg_keys = jax.random.split(jax.random.key(seed), 8)
    acts = heavy_noise(arg_keys[0], (TOKENS, D), 1.0, 6.0, ((0, 32), (1, 8)), (0, 1, 32, 2.75))
    cotan = heavy_noise(arg_keys[1], (TOKENS, D), (TOKENS ** -0.5), 0.15625, ((0, 32), (1, 8)), (0, 1, 32, 2.75))
    block_ids = with_ends(jax.random.randint(arg_keys[2], (N_DP * SAMP_BLK,), 0, POOL_BLK), jax.random.fold_in(arg_keys[2], 1), 0, POOL_BLK - 1).astype(jnp.int32)
    basis_in = gaussian(arg_keys[3], (NB, FB, FB), FB ** -0.5, 0.25, ((0, 8),))
    basis_out = gaussian(arg_keys[4], (NB, FB, FB), FB ** -0.5, 0.25)
    act_factor = draw_act_factor(jax.random.fold_in(arg_keys[7], 71), 0)
    grad_factor = draw_grad_factor(jax.random.fold_in(arg_keys[7], 71), 0)
    return {"acts": acts, "cotan": cotan, "block_ids": block_ids, "basis_in": basis_in, "basis_out": basis_out, "act_factor": act_factor, "grad_factor": grad_factor}


DECAY_RATE = 0.75
DAMPING = 0.03


def rounded(values):
    return lax.optimization_barrier(values.astype(jnp.bfloat16)).astype(jnp.float32)


def reference(acts, cotan, block_ids, basis_in, basis_out, act_factor, grad_factor):
    highest = lax.Precision.HIGHEST
    pool_rows = POOL_BLK * BLK
    act_all = acts.reshape(N_DP, pool_rows, D)
    cot_all = cotan.reshape(N_DP, pool_rows, D)
    id_rows = block_ids.reshape(N_DP, SAMP_BLK)

    def replica(carry, inputs):
        grad_total, act_total, cot_total = carry
        act_rows, cot_rows, chosen = inputs
        term = jnp.dot(cot_rows.T, act_rows, preferred_element_type=jnp.float32)
        grad_total = grad_total + rounded(term)
        act_pick = act_rows.reshape(POOL_BLK, BLK, D)[chosen].reshape(SAMP_BLK * BLK, NB, FB).astype(jnp.float32)
        cot_pick = cot_rows.reshape(POOL_BLK, BLK, D)[chosen].reshape(SAMP_BLK * BLK, NB, FB).astype(jnp.float32)
        act_term = jnp.einsum('rbi,rbj->bij', act_pick, act_pick, precision=highest) / SAMPLES
        cot_term = jnp.einsum('rbi,rbj->bij', cot_pick, cot_pick, precision=highest) * (TOKENS / SAMPLES)
        return (grad_total, act_total + act_term, cot_total + cot_term), None

    start = (jnp.zeros((D, D), jnp.float32), jnp.zeros((NB, FB, FB), jnp.float32), jnp.zeros((NB, FB, FB), jnp.float32))
    (grad_total, act_total, cot_total), _ = lax.scan(replica, start, (act_all, cot_all, id_rows))
    act_new = DECAY_RATE * act_factor + (1.0 - DECAY_RATE) * act_total
    grad_new = DECAY_RATE * grad_factor + (1.0 - DECAY_RATE) * cot_total
    basis_act = basis_in.astype(jnp.float32)
    basis_cot = basis_out.astype(jnp.float32)
    eig_in = jnp.sum(basis_act * jnp.einsum('bij,bjk->bik', act_new, basis_act, precision=highest), axis=1)
    eig_out = jnp.sum(basis_cot * jnp.einsum('bij,bjk->bik', grad_new, basis_cot, precision=highest), axis=1)
    weight_grad = grad_total.astype(jnp.bfloat16).astype(jnp.float32).reshape(NB, FB, NB, FB)
    right_side = rounded(jnp.einsum('ribj,bjk->ribk', weight_grad, basis_act, precision=highest))
    inner_term = jnp.einsum('ira,irbk->iabk', basis_cot, right_side, precision=highest)
    scaled = rounded(inner_term / (eig_out[:, :, None, None] * eig_in[None, None, :, :] + DAMPING))
    upper_term = rounded(jnp.einsum('ira,iabk->irbk', basis_cot, scaled, precision=highest))
    precond = jnp.einsum('irbk,bjk->irbj', upper_term, basis_act, precision=highest)
    return precond.reshape(D, D).astype(jnp.bfloat16), act_new, grad_new
```

```python
import jax
import jax.numpy as jnp
from jax import lax
from jax.experimental import pallas as pl
from jax.experimental.pallas import tpu as pltpu
from jax.sharding import PartitionSpec as P

MESH = pl.DeviceIdType.MESH
DECAY_RATE = 0.75
DAMPING = 0.03
BLK = 128
NX, NY, NZ = 4, 4, 8
FB = 512
PIECE = 128
HALF = 256
NF = 8
NU = 40
BF = jnp.bfloat16
F32 = jnp.float32

BATCH = {"F": (0, 8), 0: (8, 12), 1: (12, 14), 2: (14, 16), 3: (16, 18), 4: (18, 32), 5: (32, 36), 6: (36, 40)}


def tdot(a, b):
    return lax.dot_general(a, b, (((0,), (0,)), ((), ())), preferred_element_type=F32)


def ndot(a, b):
    return lax.dot_general(a, b, (((1,), (0,)), ((), ())), preferred_element_type=F32)


def device(x, y, z, c):
    return (z * 4 + (x // 2) * 2 + c, y * 2 + x % 2)


def unit_piece(i):
    j = i - NF
    late = j >= 24
    n = jnp.where(late, 12 + ((j - 24) // 4) * 2 + j % 2, j % 12)
    e = jnp.where(late, ((j - 24) % 4) // 2, j // 12)
    return n, e


def piece_source(n):
    m = n - 4
    pair = m // 2
    far = (pair == 2) | (pair == 4)
    side = m % 2
    seq = jnp.where(pair < 2, pair, (pair + 1) // 2)
    near_q = jnp.where(side == 0, (seq + 2) % 4, seq)
    far_q = side * 2 + jnp.where(pair == 4, 1, 0)
    dy = jnp.where(far, 2, jnp.where(side == 0, 1, 3))
    q = jnp.where(far, far_q, near_q)
    own = n < 4
    return jnp.where(own, 0, dy), jnp.where(own, n, q)


def kernel(
    ids, acts, cotan, basis_in, basis_out, act_factor, grad_factor,
    precond, totals,
    cotb, actb, smp, own, cout, cin, zout, ra, rb, xr, xst, wb, ts, tr, tb, fac, ebas, bout, eigb, eigs, inner, right,
    lsem, y_ss, y_rs, x_ss, x_rs, c_ss, c_rs, z_ss, a_rs, b_rs, xs_ss, xs_rs, w_ss, w_rs, t_ss, t_rs, tx_ss, tx_rs,
    tc_ss, tc_rs, e_ss, e_rs, ec_ss, ec_rs,
):
    r = lax.axis_index("dp")
    w = lax.axis_index("worker")
    z, xh, c = r // 4, (r // 2) % 2, r % 2
    y, xl = w // 2, w % 2
    x = xh * 2 + xl
    oc = 1 - c

    def at(dx=0, dy=0, dz=0):
        return device((x + dx) % NX, (y + dy) % NY, (z + dz) % NZ, c)

    core = device(x, y, z, oc)
    zp, zm, zp2, zm2 = at(dz=1), at(dz=7), at(dz=2), at(dz=6)
    yp, ym = at(dy=1), at(dy=3)
    far_x = (1 - xh) * 2 + xl
    part_x = xh * 2 + (1 - xl)
    cross_x = (1 - xh) * 2 + (1 - xl)
    partner = device(part_x, y, z, c)
    far = device(far_x, y, z, c)
    cross = device(cross_x, y, z, c)

    def rc(src, dst, ss, rs, dev):
        return pltpu.make_async_remote_copy(
            src_ref=src, dst_ref=dst, send_sem=ss, recv_sem=rs, device_id=dev, device_id_type=MESH
        )

    loads = []
    for q in range(4):
        loads.append(pltpu.make_async_copy(cotan.at[:, pl.ds(q * PIECE, PIECE)], cotb.at[q], lsem.at[q]))
    for h in range(2):
        loads.append(pltpu.make_async_copy(acts.at[:, pl.ds(h * HALF, HALF)], actb.at[xl, h], lsem.at[4 + h]))
    loads.append(pltpu.make_async_copy(basis_out.at[z], bout, lsem.at[6]))
    for cp in loads:
        cp.start()

    @pl.when(c == 0)
    def _():
        pltpu.make_async_copy(basis_in, ebas, lsem.at[7]).start()
        pltpu.make_async_copy(act_factor, fac, lsem.at[8]).start()

    @pl.when(c == 1)
    def _():
        pltpu.make_async_copy(basis_out.at[w], ebas, lsem.at[7]).start()
        pltpu.make_async_copy(grad_factor, fac, lsem.at[8]).start()

    barrier = pltpu.get_barrier_semaphore()
    for k in range(1, 8):
        wk = (w + k) % 8
        pl.semaphore_signal(barrier, inc=1, device_id=(r, wk), device_id_type=MESH)
    for dev in (core, zp, zm, zp2, zm2, far, cross):
        pl.semaphore_signal(barrier, inc=1, device_id=dev, device_id_type=MESH)
    pl.semaphore_wait(barrier, 14)

    def send_p(k):
        return rc(cotan.at[:, pl.ds(k * PIECE, PIECE)], cotb.at[(5, 7, 11, 15)[k]], y_ss.at[k], y_rs.at[(5, 7, 11, 15)[k]], yp)

    def send_m(k):
        q = (k + 2) % 4
        return rc(cotan.at[:, pl.ds(q * PIECE, PIECE)], cotb.at[(4, 6, 10, 14)[k]], y_ss.at[4 + k], y_rs.at[(4, 6, 10, 14)[k]], ym)

    def fwd_p(k):
        src, dst = (5, 7)[k], (8, 12)[k]
        return rc(cotb.at[src], cotb.at[dst], y_ss.at[8 + k], y_rs.at[dst], yp)

    def fwd_m(k):
        src, dst = (4, 6)[k], (9, 13)[k]
        return rc(cotb.at[src], cotb.at[dst], y_ss.at[10 + k], y_rs.at[dst], ym)

    def send_x(h):
        return rc(acts.at[:, pl.ds(h * HALF, HALF)], actb.at[xl, h], x_ss.at[h], x_rs.at[h], partner)

    def recv_x(h):
        return rc(acts.at[:, pl.ds(h * HALF, HALF)], actb.at[1 - xl, h], x_ss.at[h], x_rs.at[h], partner)

    for k in range(2):
        send_p(k).start()
        send_m(k).start()
        send_x(k).start()

    def wait_piece(n):
        rc(cotb.at[n], cotb.at[n], y_ss.at[0], y_rs.at[n], yp).wait_recv()

    for cp in loads[:6]:
        cp.wait()

    def target(i):
        n, _ = unit_piece(i)
        dy, _ = piece_source(n)
        return jnp.where(i < NF, i, 2 * ((y + dy) % NY) + xl)

    def dist(i):
        return (target(i) - z + NZ) % NZ

    def core_copy(i):
        return rc(cout.at[i], cin.at[i], c_ss.at[i], c_rs.at[i], core)

    def z_copy(i, dev, land, sem):
        return rc(zout.at[i], land.at[i], z_ss.at[i], sem.at[i], dev)

    def recv_a(i):
        z_copy(i, zp, ra, a_rs).wait_recv()

    def recv_b(i):
        z_copy(i, zm, rb, b_rs).wait_recv()

    def compute_factor():
        scale_own = jnp.where(c == 0, 1.0 / 8192, 4.0).astype(F32)
        scale_other = jnp.where(c == 0, 4.0, 1.0 / 8192).astype(F32)
        for s in range(2):
            into = slice(s * BLK, (s + 1) * BLK)
            for h in range(2):
                block = actb[xl, h, :BLK, :]
                for k in range(1, 8):
                    block = jnp.where(ids[s] == k, actb[xl, h, k * BLK : (k + 1) * BLK, :], block)
                smp[0, into, h * HALF : (h + 1) * HALF] = block
            for q in range(4):
                block = cotb[q, :BLK, :]
                for k in range(1, 8):
                    block = jnp.where(ids[s] == k, cotb[q, k * BLK : (k + 1) * BLK, :], block)
                smp[1, into, q * PIECE : (q + 1) * PIECE] = block

        @pl.loop(0, NF)
        def _(i):
            left = pl.ds(pl.multiple_of((i // 2) * PIECE, PIECE), PIECE)
            cols = pl.ds(pl.multiple_of((i % 2) * HALF, HALF), HALF)
            cout[i] = (tdot(smp[oc, :, left], smp[oc, :, cols]) * scale_other).astype(BF)
            core_copy(i).start()
            own[i] = tdot(smp[c, :, left], smp[c, :, cols]) * scale_own

    def compute(lo, hi):
        @pl.loop(lo, hi)
        def _(i):
            n, e = unit_piece(i)
            ea = jnp.where(e == 0, xl, 1 - xl)
            cout[i] = tdot(cotb[n], actb[ea, oc]).astype(BF)
            core_copy(i).start()
            own[i] = tdot(cotb[n], actb[ea, c])

    def merge(batch):
        lo, hi = BATCH[batch]

        @pl.loop(lo, hi)
        def _(i):
            core_copy(i).wait_recv()
            acc = own[i] + cin[i].astype(F32)
            own[i] = acc
            d = dist(i)

            @pl.when((d == 4) | (d == 5))
            def _():
                zout[i] = acc.astype(BF)

            @pl.when(d == 4)
            def _():
                z_copy(i, zp, ra, a_rs).start()

            @pl.when(d == 5)
            def _():
                z_copy(i, zm, rb, b_rs).start()

    def hop(batch, lag):
        lo, hi = BATCH[batch]

        @pl.loop(lo, hi)
        def _(i):
            d = dist(i)
            if lag < 4:
                @pl.when(d == 4 - lag)
                def _():
                    recv_a(i)
                    zout[i] = (own[i] + ra[i].astype(F32)).astype(BF)
                    z_copy(i, zp, ra, a_rs).start()

            if lag < 3:
                @pl.when(d == 5 + lag)
                def _():
                    recv_b(i)
                    zout[i] = (own[i] + rb[i].astype(F32)).astype(BF)
                    z_copy(i, zm, rb, b_rs).start()

            if lag == 4:
                @pl.when(d == 0)
                def _():
                    recv_a(i)
                    recv_b(i)
                    total = (own[i] + ra[i].astype(F32) + rb[i].astype(F32)).astype(BF)
                    if batch == "F":
                        ts[...] = total
                        rc(ts, tr, tx_ss.at[0], tx_rs.at[0], far).start()
                    else:
                        n, e = unit_piece(i)
                        _, q = piece_source(n)

                        @pl.when(e == 0)
                        def _():
                            xr[xh, q] = total
                            rc(xr.at[xh, q], xr.at[xh, q], xs_ss.at[0, q], xs_rs.at[xh, q], far).start()

                        @pl.when(e == 1)
                        def _():
                            xst[q] = total
                            rc(xst.at[q], xr.at[xh, q], xs_ss.at[1, q], xs_rs.at[xh, q], partner).start()
                            rc(xst.at[q], xr.at[xh, q], xs_ss.at[2, q], xs_rs.at[xh, q], cross).start()

    def t_copy(o, k, dev):
        return rc(tb.at[c, o], tb.at[c, o], t_ss.at[k], t_rs.at[o], dev)

    def t_core(o):
        return rc(tb.at[c, o], tb.at[c, o], tc_ss.at[o], tc_rs.at[o], core)

    def t_core_recv(o):
        return rc(tb.at[oc, o], tb.at[oc, o], tc_ss.at[o], tc_rs.at[o], core)

    def origin(dz):
        return (z + dz) % NZ

    def spread_1():
        rc(ts, tr, tx_ss.at[0], tx_rs.at[0], far).wait_recv()
        tb[c, z] = (ts[...].astype(F32) + tr[...].astype(F32)).astype(BF)
        for k, dev in enumerate((zp, zm, zp2, zm2)):
            t_copy(z, k, dev).start()
        t_core(z).start()

    def t_arrived(dz):
        o = origin(dz)
        t_copy(o, 0, zp).wait_recv()
        t_core(o).start()

    def spread_2():
        t_arrived(6)
        t_copy(origin(6), 4, zp).start()
        t_copy(origin(6), 5, zp2).start()
        t_arrived(2)
        t_copy(origin(2), 6, zm).start()
        t_arrived(7)
        t_arrived(1)

    def spread_3():
        t_arrived(5)
        t_arrived(3)
        t_arrived(4)

    def eigen():
        pltpu.make_async_copy(act_factor, fac, lsem.at[8]).wait()
        pltpu.make_async_copy(basis_in, ebas, lsem.at[7]).wait()
        eigs[...] = jnp.zeros_like(eigs)

        @pl.loop(0, 4)
        def _(q):
            rows = pl.ds(pl.multiple_of(q * PIECE, PIECE), PIECE)
            prod = jnp.zeros((PIECE, FB), F32)
            for h in range(2):
                new = (
                    DECAY_RATE * fac[rows, h * HALF : (h + 1) * HALF]
                    + (1.0 - DECAY_RATE) * tb[c, 2 * q + h].astype(F32)
                )
                basis = ebas[h * HALF : (h + 1) * HALF, :]
                for _ in range(3):
                    part = new.astype(BF)
                    prod = prod + ndot(part, basis)
                    new = new - part.astype(F32)
            prod = prod * ebas[rows, :].astype(F32)
            eigs[...] += jnp.sum(prod.reshape(PIECE // 8, 8, FB), axis=0)

        eig = jnp.broadcast_to(jnp.sum(eigs[...], axis=0, keepdims=True), (8, FB))

        @pl.when(c == 0)
        def _():
            eigb[0] = eig
            rc(eigb.at[0], eigb.at[0], ec_ss, ec_rs, core).start()

        @pl.when((c == 1) & (w == z))
        def _():
            eigb[1] = eig
            for k in range(1, 8):
                rc(eigb.at[1], eigb.at[1], e_ss.at[k - 1], e_rs, (r, (w + k) % 8)).start()

    def eigen_pass():
        @pl.when(c == 1)
        def _():
            @pl.when(w != z)
            def _():
                rc(eigb.at[1], eigb.at[1], e_ss.at[0], e_rs, (r, z)).wait_recv()

            rc(eigb.at[1], eigb.at[1], ec_ss, ec_rs, core).start()

    compute_factor()
    merge("F")
    compute(*BATCH[0])
    merge(0)
    hop("F", 1)
    wait_piece(5)
    fwd_p(0).start()
    send_p(2).start()
    wait_piece(4)
    fwd_m(0).start()
    send_m(2).start()
    compute(*BATCH[1])
    hop("F", 2)
    hop(0, 1)
    merge(1)
    hop("F", 3)
    wait_piece(7)
    fwd_p(1).start()
    send_p(3).start()
    wait_piece(6)
    fwd_m(1).start()
    send_m(3).start()
    compute(*BATCH[2])
    hop("F", 4)
    hop(0, 2)
    hop(1, 1)
    merge(2)
    spread_1()
    wait_piece(8)
    wait_piece(9)
    compute(*BATCH[3])
    hop(0, 3)
    hop(1, 2)
    hop(2, 1)
    merge(3)
    spread_2()
    recv_x(0).wait_recv()
    recv_x(1).wait_recv()
    wait_piece(11)
    wait_piece(10)
    hop(0, 4)
    hop(1, 3)
    hop(2, 2)
    hop(3, 1)
    compute(*BATCH[4])
    merge(4)
    spread_3()
    wait_piece(12)
    wait_piece(13)
    hop(1, 4)
    hop(2, 3)
    hop(3, 2)
    hop(4, 1)
    compute(*BATCH[5])
    merge(5)
    eigen()
    wait_piece(15)
    wait_piece(14)
    compute(*BATCH[6])
    hop(2, 4)
    hop(3, 3)
    hop(4, 2)
    hop(5, 1)
    merge(6)
    eigen_pass()
    hop(3, 4)
    hop(4, 3)
    hop(5, 2)
    hop(6, 1)
    for o in range(NF):
        t_core_recv(o).wait_recv()
    for f in range(2):
        for o in range(NF):
            pltpu.make_async_copy(
                tb.at[f, o],
                totals.at[f, pl.ds((o // 2) * PIECE, PIECE), pl.ds((o % 2) * HALF, HALF)],
                lsem.at[9 + f * NF + o],
            ).start()
    hop(4, 4)
    hop(5, 3)
    hop(6, 2)
    hop(5, 4)
    hop(6, 3)
    hop(6, 4)

    pltpu.make_async_copy(basis_out.at[z], bout, lsem.at[6]).wait()
    inner[...] = jnp.zeros_like(inner)

    def w_copy(h, q):
        return rc(wb.at[h, q], wb.at[h, q], w_ss.at[q], w_rs.at[q], core)

    home = (z % 2) == xl

    @pl.loop(0, 4)
    def _(q):
        @pl.when(jnp.logical_not(home))
        def _():
            rc(xst.at[q], xr.at[xh, q], xs_ss.at[0, q], xs_rs.at[xh, q], far).wait_recv()

        rc(xst.at[q], xr.at[1 - xh, q], xs_ss.at[0, q], xs_rs.at[1 - xh, q], far).wait_recv()
        wb[c, q] = (xr[0, q].astype(F32) + xr[1, q].astype(F32)).astype(BF)
        w_copy(c, q).start()

    @pl.loop(0, 4)
    def _(q):
        w_copy(oc, q).wait_recv()
        right[...] = (ndot(wb[0, q], basis_in[:HALF, :]) + ndot(wb[1, q], basis_in[HALF:, :])).astype(BF)
        rows = pl.ds(pl.multiple_of(q * PIECE, PIECE), PIECE)
        inner[...] += tdot(bout[rows, :], right[...])

    @pl.when(c == 0)
    def _():
        rc(eigb.at[1], eigb.at[1], ec_ss, ec_rs, core).wait_recv()

    @pl.when(c == 1)
    def _():
        rc(eigb.at[0], eigb.at[0], ec_ss, ec_rs, core).wait_recv()

    ei = eigb[0, 0:1, :]
    eo = jnp.transpose(jnp.broadcast_to(eigb[1, 0:1, :], (PIECE, FB)))
    eo = jnp.concatenate([eo] * 4, axis=1)
    scaled = (inner[...] / (eo * ei + DAMPING)).astype(BF)
    mine = pl.ds(pl.multiple_of((xh * 2 + c) * PIECE, PIECE), PIECE)
    upper = ndot(bout[mine, :], scaled).astype(BF)
    precond[...] = lax.dot_general(
        upper, basis_in[...], (((1,), (1,)), ((), ())), preferred_element_type=F32
    ).astype(BF)

    for k in range(4):
        send_p(k).wait_send()
        send_m(k).wait_send()
    for k in range(2):
        fwd_p(k).wait_send()
        fwd_m(k).wait_send()
        send_x(k).wait_send()

    @pl.loop(0, NU)
    def _(i):
        core_copy(i).wait_send()

        @pl.when(dist(i) != 0)
        def _():
            z_copy(i, zp, ra, a_rs).wait_send()

    rc(ts, tr, tx_ss.at[0], tx_rs.at[0], far).wait_send()
    for k in range(7):
        t_copy(z, k, zp).wait_send()
    for o in range(NF):
        t_core(o).wait_send()

    @pl.when(home)
    def _():
        for k in range(3):
            for q in range(4):
                rc(xst.at[q], xr.at[xh, q], xs_ss.at[k, q], xs_rs.at[xh, q], far).wait_send()

    for q in range(4):
        w_copy(c, q).wait_send()
    rc(eigb.at[0], eigb.at[0], ec_ss, ec_rs, core).wait_send()

    @pl.when((c == 1) & (w == z))
    def _():
        for k in range(1, 8):
            rc(eigb.at[1], eigb.at[1], e_ss.at[k - 1], e_rs, (r, (w + k) % 8)).wait_send()

    for f in range(2):
        for o in range(NF):
            pltpu.make_async_copy(
                tb.at[f, o],
                totals.at[f, pl.ds((o // 2) * PIECE, PIECE), pl.ds((o % 2) * HALF, HALF)],
                lsem.at[9 + f * NF + o],
            ).wait()


def per_device(acts, cotan, block_ids, basis_in, basis_out, act_factor, grad_factor):
    vm = pltpu.VMEM
    dma = pltpu.SemaphoreType.DMA
    unit = (PIECE, HALF)
    any_spec = pl.BlockSpec(memory_space=pl.ANY)
    precond, totals = pl.pallas_call(
        kernel,
        name="kfac",
        out_shape=(
            jax.ShapeDtypeStruct((PIECE, FB), BF),
            jax.ShapeDtypeStruct((2, FB, FB), BF),
        ),
        in_specs=[
            pl.BlockSpec(memory_space=pltpu.SMEM),
            any_spec,
            any_spec,
            pl.BlockSpec(memory_space=pltpu.VMEM),
            any_spec,
            any_spec,
            any_spec,
        ],
        out_specs=(pl.BlockSpec(memory_space=pltpu.VMEM), any_spec),
        scratch_shapes=[
            vm((16, 1024, PIECE), BF),
            vm((2, 2, 1024, HALF), BF),
            vm((2, 2 * BLK, FB), BF),
            vm((NU,) + unit, F32),
            vm((NU,) + unit, BF),
            vm((NU,) + unit, BF),
            vm((NU,) + unit, BF),
            vm((NU,) + unit, BF),
            vm((NU,) + unit, BF),
            vm((2, 4) + unit, BF),
            vm((4,) + unit, BF),
            vm((2, 4) + unit, BF),
            vm(unit, BF),
            vm(unit, BF),
            vm((2, NF) + unit, BF),
            vm((FB, FB), F32),
            vm((FB, FB), BF),
            vm((FB, FB), BF),
            vm((2, 8, FB), F32),
            vm((8, FB), F32),
            vm((FB, FB), F32),
            vm((PIECE, FB), BF),
            dma((25,)),
            dma((12,)),
            dma((16,)),
            dma((2,)),
            dma((2,)),
            dma((NU,)),
            dma((NU,)),
            dma((NU,)),
            dma((NU,)),
            dma((NU,)),
            dma((3, 4)),
            dma((2, 4)),
            dma((4,)),
            dma((4,)),
            dma((7,)),
            dma((NF,)),
            dma((1,)),
            dma((1,)),
            dma((NF,)),
            dma((NF,)),
            dma((7,)),
            dma,
            dma,
            dma,
        ],
        compiler_params=pltpu.CompilerParams(
            collective_id=0, has_side_effects=True, vmem_limit_bytes=48 << 20
        ),
    )(
        block_ids,
        acts,
        cotan,
        basis_in.reshape(FB, FB),
        basis_out,
        act_factor.reshape(FB, FB),
        grad_factor.reshape(FB, FB),
    )
    totals = totals.astype(F32)
    act_new = DECAY_RATE * act_factor + (1.0 - DECAY_RATE) * totals[0:1]
    grad_new = DECAY_RATE * grad_factor + (1.0 - DECAY_RATE) * totals[1:2]
    return precond, act_new, grad_new


def solution(mesh):
    return jax.shard_map(
        per_device,
        mesh=mesh,
        in_specs=(
            P("dp", "worker"),
            P("dp", "worker"),
            P("dp"),
            P("worker", None, None),
            P(),
            P("worker", None, None),
            P("worker", None, None),
        ),
        out_specs=(P("dp", "worker"), P("worker", None, None), P("worker", None, None)),
        check_vma=False,
    )
```

```python
import jax
import jax.numpy as jnp
from jax import lax
from jax.experimental import pallas as pl
from jax.experimental.pallas import tpu as pltpu
from jax.sharding import PartitionSpec as P

MESH = pl.DeviceIdType.MESH
DECAY_RATE = 0.75
DAMPING = 0.03
BLK = 128
NX, NY, NZ = 4, 4, 8
FB = 512
PIECE = 128
HALF = 256
NF = 8
NU = 40
TREE_FROM = 40
BF = jnp.bfloat16
F32 = jnp.float32


def tdot(a, b):
    return lax.dot_general(a, b, (((0,), (0,)), ((), ())), preferred_element_type=F32)


def ndot(a, b):
    return lax.dot_general(a, b, (((1,), (0,)), ((), ())), preferred_element_type=F32)


def device(x, y, z, c):
    return (z * 4 + (x // 2) * 2 + c, y * 2 + x % 2)


def unit_parts(i):
    j = i - NF
    runs = (
        (0, 0, 0, None),
        (8, 0, 1, 0),
        (12, 4, 0, None),
        (14, 4, 1, 0),
        (15, 5, 0, None),
        (17, 5, 1, 0),
        (18, 0, 1, 1),
    )
    m, e, h = j, j, j
    for lo, pair, acts, half in runs:
        here = j >= lo
        m = jnp.where(here, pair + ((j - lo) // 2 if half is None else j - lo), m)
        e = jnp.where(here, acts, e)
        h = jnp.where(here, (j - lo) % 2 if half is None else half, h)
    late = j >= 24
    m = jnp.where(late, 6 + (j - 24) // 4, m)
    e = jnp.where(late, (j // 2) % 2, e)
    h = jnp.where(late, j % 2, h)
    return m, e, h


def kept_piece(m, c):
    return 2 * m + jnp.where((m == 3) | (m == 7), 1 - c, c)


def piece_source(n):
    m = n // 2
    far = (m == 4) | (m == 6)
    k = jnp.where(m < 2, 0, jnp.where(far, 3, 1 + n % 2))
    far_idx = jnp.where(m == 6, 2, 0) + n % 2
    idx = jnp.where(m < 2, n, jnp.where(far, far_idx, jnp.where(m < 4, m - 2, (m - 1) // 2)))
    return k, idx


def feature_block(k, idx):
    return jnp.where(k == 3, (idx % 2) * 2 + idx // 2, jnp.where(k == 1, (idx + 2) % 4, idx))


def y_offset(k):
    return jnp.where(k == 2, 3, jnp.where(k == 3, 2, k))


def kernel(
    ids, acts, cotan, basis_in, basis_out, act_factor, grad_factor,
    precond, act_new, grad_new,
    cotb, actb, smp, own, cout, cin, zout, ra, rb, rcc, rd, xr, xst, wb, ts, tr, tb, fac, ebas, bout, eigb, eigs, scaled, right,
    lsem, y_ss, y_rs, x_ss, x_rs, c_ss, c_rs, z_ss, a_rs, b_rs, cc_rs, d_rs, xs_ss, xs_rs, w_ss, w_rs, t_ss, t_rs, tx_ss, tx_rs,
    tc_ss, tc_rs, e_ss, e_rs, ec_ss, ec_rs,
):
    r = lax.axis_index("dp")
    w = lax.axis_index("worker")
    z, xh, c = r // 4, (r // 2) % 2, r % 2
    y, xl = w // 2, w % 2
    x = xh * 2 + xl
    oc = 1 - c

    def at(dx=0, dy=0, dz=0):
        return device((x + dx) % NX, (y + dy) % NY, (z + dz) % NZ, c)

    core = device(x, y, z, oc)
    zp, zm, zp2, zm2 = at(dz=1), at(dz=7), at(dz=2), at(dz=6)
    yp, ym = at(dy=1), at(dy=3)
    far_x = (1 - xh) * 2 + xl
    part_x = xh * 2 + (1 - xl)
    cross_x = (1 - xh) * 2 + (1 - xl)
    partner = device(part_x, y, z, c)
    far = device(far_x, y, z, c)
    cross = device(cross_x, y, z, c)

    def rc(src, dst, ss, rs, dev):
        return pltpu.make_async_remote_copy(
            src_ref=src, dst_ref=dst, send_sem=ss, recv_sem=rs, device_id=dev, device_id_type=MESH
        )

    loads = []
    for q in range(4):
        into = cotb.at[q // 2, :, pl.ds((q % 2) * PIECE, PIECE)]
        loads.append(pltpu.make_async_copy(cotan.at[:, pl.ds(q * PIECE, PIECE)], into, lsem.at[q]))
    for h in range(2):
        loads.append(pltpu.make_async_copy(acts.at[:, pl.ds(h * HALF, HALF)], actb.at[xl, h], lsem.at[4 + h]))
    loads.append(pltpu.make_async_copy(basis_out.at[z], bout, lsem.at[6]))
    for cp in loads:
        cp.start()

    @pl.when(c == 0)
    def _():
        pltpu.make_async_copy(basis_in, ebas, lsem.at[7]).start()

    @pl.when(c == 1)
    def _():
        pltpu.make_async_copy(basis_out.at[w], ebas, lsem.at[7]).start()

    factor_loads = [
        pltpu.make_async_copy(act_factor, fac.at[0], lsem.at[8]),
        pltpu.make_async_copy(grad_factor, fac.at[1], lsem.at[9]),
    ]
    for cp in factor_loads:
        cp.start()

    barrier = pltpu.get_barrier_semaphore()
    for k in range(1, 8):
        wk = (w + k) % 8
        pl.semaphore_signal(barrier, inc=1, device_id=(r, wk), device_id_type=MESH)
    for dev in (core, zp, zm, zp2, zm2, far, cross):
        pl.semaphore_signal(barrier, inc=1, device_id=dev, device_id_type=MESH)
    pl.semaphore_wait(barrier, 14)

    def piece(n):
        return cotb.at[n // 2, :, pl.ds((n % 2) * PIECE, PIECE)]

    def send_p(k):
        n = (5, 7, 11, 15)[k]
        return rc(cotan.at[:, pl.ds(k * PIECE, PIECE)], piece(n), y_ss.at[k], y_rs.at[n], yp)

    def send_m(k):
        n = (4, 6, 10, 14)[k]
        q = (k + 2) % 4
        return rc(cotan.at[:, pl.ds(q * PIECE, PIECE)], piece(n), y_ss.at[4 + k], y_rs.at[n], ym)

    def fwd_p(k):
        src, dst = (5, 7)[k], (8, 12)[k]
        return rc(piece(src), piece(dst), y_ss.at[8 + k], y_rs.at[dst], yp)

    def fwd_m(k):
        src, dst = (4, 6)[k], (9, 13)[k]
        return rc(piece(src), piece(dst), y_ss.at[10 + k], y_rs.at[dst], ym)

    def send_x(h):
        return rc(acts.at[:, pl.ds(h * HALF, HALF)], actb.at[xl, h], x_ss.at[h], x_rs.at[h], partner)

    def recv_x(h):
        return rc(acts.at[:, pl.ds(h * HALF, HALF)], actb.at[1 - xl, h], x_ss.at[h], x_rs.at[h], partner)

    for k in range(2):
        send_p(k).start()
        send_m(k).start()
        send_x(k).start()

    def wait_piece(n):
        rc(piece(n), piece(n), y_ss.at[0], y_rs.at[n], yp).wait_recv()

    for cp in loads[:6]:
        cp.wait()

    def dist(i):
        k, _ = piece_source(kept_piece(unit_parts(i)[0], c))
        to = jnp.where(i < NF, i, 2 * ((y + y_offset(k)) % NY) + xl)
        return (to - z + NZ) % NZ

    def core_copy(i):
        return rc(cout.at[i], cin.at[i], c_ss.at[i], c_rs.at[i], core)

    def z_copy(i, dev, land, sem):
        return rc(zout.at[i], land.at[i], z_ss.at[i], sem.at[i], dev)

    lands = {"a": (ra, a_rs), "b": (rb, b_rs), "c": (rcc, cc_rs), "d": (rd, d_rs)}

    def send_z(i, dev, slot):
        z_copy(i, dev, *lands[slot]).start()

    def recv_z(i, slots):
        for slot in slots:
            z_copy(i, zp, *lands[slot]).wait_recv()
        acc = own[i]
        for slot in slots:
            acc = acc + lands[slot][0][i].astype(F32)
        return acc.astype(BF)

    def compute_factor():
        scale_own = jnp.where(c == 0, 1.0 / 8192, 4.0).astype(F32)
        scale_other = jnp.where(c == 0, 4.0, 1.0 / 8192).astype(F32)
        for s in range(2):
            into = slice(s * BLK, (s + 1) * BLK)
            for h in range(2):
                block = actb[xl, h, :BLK, :]
                for k in range(1, 8):
                    block = jnp.where(ids[s] == k, actb[xl, h, k * BLK : (k + 1) * BLK, :], block)
                smp[0, into, h * HALF : (h + 1) * HALF] = block
            for q in range(4):
                cols = slice((q % 2) * PIECE, (q % 2 + 1) * PIECE)
                block = cotb[q // 2, :BLK, cols]
                for k in range(1, 8):
                    block = jnp.where(ids[s] == k, cotb[q // 2, k * BLK : (k + 1) * BLK, cols], block)
                smp[1, into, q * PIECE : (q + 1) * PIECE] = block

        @pl.loop(0, NF)
        def _(i):
            left = pl.ds(pl.multiple_of((i // 2) * PIECE, PIECE), PIECE)
            cols = pl.ds(pl.multiple_of((i % 2) * HALF, HALF), HALF)
            cout[i] = (tdot(smp[oc, :, left], smp[oc, :, cols]) * scale_other).astype(BF)
            core_copy(i).start()
            own[i] = tdot(smp[c, :, left], smp[c, :, cols]) * scale_own

    def compute(i):
        m, e, h = unit_parts(i)
        ea = jnp.where(e == 0, xl, 1 - xl)
        both = tdot(cotb[m], actb[ea, h])
        lower = kept_piece(m, c) % 2 == 0
        cout[i] = jnp.where(lower, both[PIECE:], both[:PIECE]).astype(BF)
        core_copy(i).start()
        own[i] = jnp.where(lower, both[:PIECE], both[PIECE:])

    def is_tree(i):
        return (i >= TREE_FROM) | (i < NF)

    def merge(i):
        core_copy(i).wait_recv()
        acc = own[i] + cin[i].astype(F32)
        own[i] = acc
        d = dist(i)
        tree = is_tree(i)
        far_up = d == 4
        far_down = d == 5
        near_up = tree & ((d == 1) | (d == 3))
        near_down = tree & (d == 7)

        @pl.when(far_up | far_down | near_up | near_down)
        def _():
            zout[i] = acc.astype(BF)

        @pl.when(far_up & tree)
        def _():
            send_z(i, zp2, "a")

        @pl.when((far_up & jnp.logical_not(tree)) | (near_up & (d == 1)))
        def _():
            send_z(i, zp, "a")

        @pl.when(near_up & (d == 3))
        def _():
            send_z(i, zp, "b")

        @pl.when(far_down | near_down)
        def _():
            send_z(i, zm, "b")

    def pass_on(i, cond, slots, dev, slot):
        @pl.when(cond)
        def _():
            zout[i] = recv_z(i, slots)
            send_z(i, dev, slot)

    def finish_z(i, cond, slots):
        @pl.when(cond)
        def _():
            total = recv_z(i, slots)

            @pl.when(i < NF)
            def _():
                ts[...] = total
                rc(ts, tr, tx_ss.at[0], tx_rs.at[0], far).start()

            @pl.when(i >= NF)
            def _():
                m, e, h = unit_parts(i)
                q = feature_block(*piece_source(kept_piece(m, c)))

                @pl.when(e == 0)
                def _():
                    xr[xh, q, h] = total
                    rc(xr.at[xh, q, h], xr.at[xh, q, h], xs_ss.at[0, q, h], xs_rs.at[xh, q, h], far).start()

                @pl.when(e == 1)
                def _():
                    xst[q, h] = total
                    rc(xst.at[q, h], xr.at[xh, q, h], xs_ss.at[1, q, h], xs_rs.at[xh, q, h], partner).start()
                    rc(xst.at[q, h], xr.at[xh, q, h], xs_ss.at[2, q, h], xs_rs.at[xh, q, h], cross).start()

    def hop_1(i):
        d, tree = dist(i), is_tree(i)
        chain = jnp.logical_not(tree)
        pass_on(i, (d == 3) & chain, "a", zp, "a")
        pass_on(i, (d == 6) & chain, "b", zm, "b")
        pass_on(i, (d == 2) & tree, "ab", zp2, "c")
        pass_on(i, (d == 6) & tree, "b", zm2, "d")

    def hop_2(i):
        d, tree = dist(i), is_tree(i)
        chain = jnp.logical_not(tree)
        pass_on(i, (d == 2) & chain, "a", zp, "a")
        pass_on(i, (d == 7) & chain, "b", zm, "b")
        finish_z(i, (d == 0) & tree, "abcd")

    def hop_3(i):
        pass_on(i, (dist(i) == 1) & jnp.logical_not(is_tree(i)), "a", zp, "a")

    def hop_4(i):
        finish_z(i, (dist(i) == 0) & jnp.logical_not(is_tree(i)), "ab")

    stages = (compute, merge, hop_1, hop_2, hop_3, hop_4)
    done = [NF] * len(stages)

    def advance(stage, to):
        lo, to = done[stage], min(to, NU)
        if to > lo:
            pl.loop(lo, to)(stages[stage])
            done[stage] = to

    def advance_all(to, lags):
        for stage in range(len(stages) - 1, 0, -1):
            advance(stage, to - lags[stage])

    def run(to, lags):
        lo = done[0]
        advance_all(lo, lags)

        @pl.loop(lo, to)
        def _(i):
            compute(i)
            for stage in range(1, len(stages)):
                first, lag = done[stage], lags[stage]
                if to - lag > first:
                    if lo - lag >= first:
                        stages[stage](i - lag)
                    else:
                        pl.when(i - lag >= first)(lambda stage=stage, lag=lag: stages[stage](i - lag))

        done[0] = to
        for stage in range(1, len(stages)):
            done[stage] = max(done[stage], to - lags[stage])

    def each_factor(step):
        pl.loop(0, NF)(step)

    def t_copy(o, k, dev):
        return rc(tb.at[c, o], tb.at[c, o], t_ss.at[k], t_rs.at[o], dev)

    def t_core(o):
        return rc(tb.at[c, o], tb.at[c, o], tc_ss.at[o], tc_rs.at[o], core)

    def t_core_recv(o):
        return rc(tb.at[oc, o], tb.at[oc, o], tc_ss.at[o], tc_rs.at[o], core)

    def origin(dz):
        return (z + dz) % NZ

    def spread_1():
        rc(ts, tr, tx_ss.at[0], tx_rs.at[0], far).wait_recv()
        tb[c, z] = (ts[...].astype(F32) + tr[...].astype(F32)).astype(BF)
        for k, dev in enumerate((zp, zm, zp2, zm2)):
            t_copy(z, k, dev).start()
        t_core(z).start()

    def t_arrived(dz):
        o = origin(dz)
        t_copy(o, 0, zp).wait_recv()
        t_core(o).start()

    def spread_2():
        t_arrived(6)
        t_copy(origin(6), 4, zp).start()
        t_copy(origin(6), 5, zp2).start()
        t_arrived(2)
        t_copy(origin(2), 6, zm).start()
        t_arrived(7)
        t_arrived(1)

    def spread_3():
        t_arrived(5)
        t_arrived(3)
        t_arrived(4)

    def new_factor(f, q, h):
        rows, cols = slice(q * PIECE, (q + 1) * PIECE), slice(h * HALF, (h + 1) * HALF)
        return DECAY_RATE * fac[f, rows, cols] + (1.0 - DECAY_RATE) * tb[f, 2 * q + h].astype(F32)

    def eigen_start():
        for cp in factor_loads:
            cp.wait()
        pltpu.make_async_copy(basis_in, ebas, lsem.at[7]).wait()
        eigs[...] = jnp.zeros_like(eigs)

    def eigen_rows(q):
        rows = slice(q * PIECE, (q + 1) * PIECE)
        prod = jnp.zeros((PIECE, FB), F32)
        for h in range(2):
            new = DECAY_RATE * fac[c, rows, h * HALF : (h + 1) * HALF] + (1.0 - DECAY_RATE) * tb[
                c, 2 * q + h
            ].astype(F32)
            basis = ebas[h * HALF : (h + 1) * HALF, :]
            for _ in range(3):
                part = new.astype(BF)
                prod = prod + ndot(part, basis)
                new = new - part.astype(F32)
        prod = prod * ebas[rows, :].astype(F32)
        eigs[...] += jnp.sum(prod.reshape(PIECE // 8, 8, FB), axis=0)

    def factor_outputs():
        for o in range(NF):
            t_core_recv(o).wait_recv()
        for q in range(4):
            for h in range(2):
                rows, cols = slice(q * PIECE, (q + 1) * PIECE), slice(h * HALF, (h + 1) * HALF)
                act_new[rows, cols] = new_factor(0, q, h)
                grad_new[rows, cols] = new_factor(1, q, h)

    def eigen_end():
        eig = jnp.broadcast_to(jnp.sum(eigs[...], axis=0, keepdims=True), (8, FB))

        @pl.when(c == 0)
        def _():
            eigb[0] = eig
            rc(eigb.at[0], eigb.at[0], ec_ss, ec_rs, core).start()

        @pl.when((c == 1) & (w == z))
        def _():
            eigb[1] = eig
            for k in range(1, 8):
                rc(eigb.at[1], eigb.at[1], e_ss.at[k - 1], e_rs, (r, (w + k) % 8)).start()

    def eigen_pass():
        @pl.when(c == 1)
        def _():
            @pl.when(w != z)
            def _():
                rc(eigb.at[1], eigb.at[1], e_ss.at[0], e_rs, (r, z)).wait_recv()

            rc(eigb.at[1], eigb.at[1], ec_ss, ec_rs, core).start()

    lags = (0, 2, 7, 12, 17, 22)
    compute_factor()
    each_factor(merge)
    run(12, lags)
    advance(1, 12)
    each_factor(hop_1)
    wait_piece(5)
    fwd_p(0).start()
    send_p(2).start()
    wait_piece(4)
    fwd_m(0).start()
    send_m(2).start()
    run(14, lags)
    advance(1, 14)
    advance(2, 12)
    each_factor(hop_2)
    wait_piece(7)
    fwd_p(1).start()
    send_p(3).start()
    wait_piece(6)
    fwd_m(1).start()
    send_m(3).start()
    run(16, lags)
    recv_x(0).wait_recv()
    run(20, lags)
    advance(1, 20)
    advance(3, 12)
    advance(2, 14)
    spread_1()
    wait_piece(8)
    wait_piece(9)
    run(23, lags)
    advance(1, 23)
    advance(4, 12)
    advance(3, 14)
    advance(2, 20)
    spread_2()
    wait_piece(10)
    wait_piece(11)
    run(26, lags)
    recv_x(1).wait_recv()
    run(32, lags)
    spread_3()
    wait_piece(12)
    wait_piece(13)
    run(36, lags)
    wait_piece(14)
    wait_piece(15)
    run(40, lags)
    advance(1, 40)
    eigen_start()
    for to in range(41, 40 + 23):
        advance_all(to, lags)
        if to in (42, 45, 48, 51):
            eigen_rows((to - 42) // 3)
        if to == 51:
            eigen_end()
        if to == 56:
            factor_outputs()
    eigen_pass()

    pltpu.make_async_copy(basis_out.at[z], bout, lsem.at[6]).wait()
    def w_copy(q):
        return rc(wb.at[q], wb.at[q], w_ss.at[q], w_rs.at[q], core)

    home = (z % 2) == xl
    dy = (z // 2 - y + NY) % NY
    shard = jnp.where(dy == 3, 2, jnp.where(dy == 2, 3, dy))

    def mine_first(idx):
        return jnp.where(shard == 2, 1 - idx % 2, idx % 2) == c

    @pl.loop(0, 4)
    def _(idx):
        q = feature_block(shard, idx)

        @pl.when(mine_first(idx))
        def _():
            for h in range(2):
                @pl.when(jnp.logical_not(home))
                def _():
                    rc(xst.at[q, h], xr.at[xh, q, h], xs_ss.at[0, q, h], xs_rs.at[xh, q, h], far).wait_recv()

                rc(xst.at[q, h], xr.at[1 - xh, q, h], xs_ss.at[0, q, h], xs_rs.at[1 - xh, q, h], far).wait_recv()
                wb[q, :, h * HALF : (h + 1) * HALF] = (
                    xr[0, q, h].astype(F32) + xr[1, q, h].astype(F32)
                ).astype(BF)
            w_copy(q).start()

    @pl.loop(0, 4)
    def _(idx):
        q = feature_block(shard, idx)

        @pl.when(jnp.logical_not(mine_first(idx)))
        def _():
            w_copy(q).wait_recv()

        rows = pl.ds(pl.multiple_of(q * PIECE, PIECE), PIECE)
        right[rows, :] = ndot(wb[q], basis_in[...]).astype(BF)

    @pl.when(c == 0)
    def _():
        rc(eigb.at[1], eigb.at[1], ec_ss, ec_rs, core).wait_recv()

    @pl.when(c == 1)
    def _():
        rc(eigb.at[0], eigb.at[0], ec_ss, ec_rs, core).wait_recv()

    ei = eigb[0, 0:1, :]
    for a in range(4):
        rows = slice(a * PIECE, (a + 1) * PIECE)
        eo = jnp.transpose(jnp.broadcast_to(eigb[1, 0:1, rows], (PIECE, PIECE)))
        eo = jnp.concatenate([eo] * 4, axis=1)
        scaled[rows, :] = (tdot(bout[:, rows], right[...]) / (eo * ei + DAMPING)).astype(BF)
    mine = pl.ds(pl.multiple_of((xh * 2 + c) * PIECE, PIECE), PIECE)
    upper = ndot(bout[mine, :], scaled[...]).astype(BF)
    precond[...] = lax.dot_general(
        upper, basis_in[...], (((1,), (1,)), ((), ())), preferred_element_type=F32
    ).astype(BF)

    for k in range(4):
        send_p(k).wait_send()
        send_m(k).wait_send()
    for k in range(2):
        fwd_p(k).wait_send()
        fwd_m(k).wait_send()
        send_x(k).wait_send()

    @pl.loop(0, NU)
    def _(i):
        core_copy(i).wait_send()

        @pl.when(dist(i) != 0)
        def _():
            z_copy(i, zp, ra, a_rs).wait_send()

    rc(ts, tr, tx_ss.at[0], tx_rs.at[0], far).wait_send()
    for k in range(7):
        t_copy(z, k, zp).wait_send()
    for o in range(NF):
        t_core(o).wait_send()

    @pl.when(home)
    def _():
        @pl.loop(0, 4)
        def _(idx):
            q = feature_block(shard, idx)

            @pl.when(mine_first(idx))
            def _():
                for k in range(3):
                    for h in range(2):
                        rc(
                            xst.at[q, h], xr.at[xh, q, h], xs_ss.at[k, q, h], xs_rs.at[xh, q, h], far
                        ).wait_send()

    @pl.loop(0, 4)
    def _(idx):
        @pl.when(mine_first(idx))
        def _():
            w_copy(feature_block(shard, idx)).wait_send()

    rc(eigb.at[0], eigb.at[0], ec_ss, ec_rs, core).wait_send()

    @pl.when((c == 1) & (w == z))
    def _():
        for k in range(1, 8):
            rc(eigb.at[1], eigb.at[1], e_ss.at[k - 1], e_rs, (r, (w + k) % 8)).wait_send()


def per_device(acts, cotan, block_ids, basis_in, basis_out, act_factor, grad_factor):
    vm = pltpu.VMEM
    dma = pltpu.SemaphoreType.DMA
    unit = (PIECE, HALF)
    any_spec = pl.BlockSpec(memory_space=pltpu.HBM)
    precond, act_new, grad_new = pl.pallas_call(
        kernel,
        name="kfac",
        out_shape=(
            jax.ShapeDtypeStruct((PIECE, FB), BF),
            jax.ShapeDtypeStruct((FB, FB), F32),
            jax.ShapeDtypeStruct((FB, FB), F32),
        ),
        in_specs=[
            pl.BlockSpec(memory_space=pltpu.SMEM),
            any_spec,
            any_spec,
            pl.BlockSpec(memory_space=pltpu.VMEM),
            any_spec,
            any_spec,
            any_spec,
        ],
        out_specs=(pl.BlockSpec(memory_space=pltpu.VMEM),) * 3,
        scratch_shapes=[
            vm((8, 1024, HALF), BF),
            vm((2, 2, 1024, HALF), BF),
            vm((2, 2 * BLK, FB), BF),
            vm((NU,) + unit, F32),
            vm((NU,) + unit, BF),
            vm((NU,) + unit, BF),
            vm((NU,) + unit, BF),
            vm((NU,) + unit, BF),
            vm((NU,) + unit, BF),
            vm((NU,) + unit, BF),
            vm((NU,) + unit, BF),
            vm((2, 4, 2) + unit, BF),
            vm((4, 2) + unit, BF),
            vm((4, PIECE, FB), BF),
            vm(unit, BF),
            vm(unit, BF),
            vm((2, NF) + unit, BF),
            vm((2, FB, FB), F32),
            vm((FB, FB), BF),
            vm((FB, FB), BF),
            vm((2, 8, FB), F32),
            vm((8, FB), F32),
            vm((FB, FB), BF),
            vm((FB, FB), BF),
            dma((10,)),
            dma((12,)),
            dma((16,)),
            dma((2,)),
            dma((2,)),
            dma((NU,)),
            dma((NU,)),
            dma((NU,)),
            dma((NU,)),
            dma((NU,)),
            dma((NU,)),
            dma((NU,)),
            dma((3, 4, 2)),
            dma((2, 4, 2)),
            dma((4,)),
            dma((4,)),
            dma((7,)),
            dma((NF,)),
            dma((1,)),
            dma((1,)),
            dma((NF,)),
            dma((NF,)),
            dma((7,)),
            dma,
            dma,
            dma,
        ],
        compiler_params=pltpu.CompilerParams(
            collective_id=0, has_side_effects=True, vmem_limit_bytes=60 << 20
        ),
    )(
        block_ids,
        acts,
        cotan,
        basis_in.reshape(FB, FB),
        basis_out,
        act_factor.reshape(FB, FB),
        grad_factor.reshape(FB, FB),
    )
    return precond, act_new.reshape(1, FB, FB), grad_new.reshape(1, FB, FB)


def solution(mesh):
    return jax.shard_map(
        per_device,
        mesh=mesh,
        in_specs=(
            P("dp", "worker"),
            P("dp", "worker"),
            P("dp"),
            P("worker", None, None),
            P(),
            P("worker", None, None),
            P("worker", None, None),
        ),
        out_specs=(P("dp", "worker"), P("worker", None, None), P("worker", None, None)),
        check_vma=False,
    )
```

```python
import jax
import jax.numpy as jnp
from jax import lax
from jax.experimental import pallas as pl
from jax.experimental.pallas import tpu as pltpu
from jax.sharding import PartitionSpec as P

MESH = pl.DeviceIdType.MESH
DECAY_RATE = 0.75
DAMPING = 0.03
BLK = 128
NX, NY, NZ = 4, 4, 8
FB = 512
PIECE = 128
HALF = 256
NF = 8
NU = 40
SKIP_FROM = 36
BF = jnp.bfloat16
F32 = jnp.float32


def tdot(a, b):
    return lax.dot_general(a, b, (((0,), (0,)), ((), ())), preferred_element_type=F32)


def ndot(a, b):
    return lax.dot_general(a, b, (((1,), (0,)), ((), ())), preferred_element_type=F32)


def device(x, y, z, c):
    return (z * 4 + (x // 2) * 2 + c, y * 2 + x % 2)


def unit_parts(i):
    j = i - NF
    runs = (
        (0, 0, 0, None),
        (8, 0, 1, 0),
        (12, 4, 0, None),
        (14, 4, 1, 0),
        (15, 5, 0, None),
        (17, 5, 1, 0),
        (18, 0, 1, 1),
    )
    m, e, h = j, j, j
    for lo, pair, acts, half in runs:
        here = j >= lo
        m = jnp.where(here, pair + ((j - lo) // 2 if half is None else j - lo), m)
        e = jnp.where(here, acts, e)
        h = jnp.where(here, (j - lo) % 2 if half is None else half, h)
    late = j >= 24
    m = jnp.where(late, 6 + (j - 24) // 4, m)
    e = jnp.where(late, (j // 2) % 2, e)
    h = jnp.where(late, j % 2, h)
    return m, e, h


def kept_piece(m, c):
    return 2 * m + jnp.where((m == 3) | (m == 7), 1 - c, c)


def piece_source(n):
    m = n // 2
    far = (m == 4) | (m == 6)
    k = jnp.where(m < 2, 0, jnp.where(far, 3, 1 + n % 2))
    far_idx = jnp.where(m == 6, 2, 0) + n % 2
    idx = jnp.where(m < 2, n, jnp.where(far, far_idx, jnp.where(m < 4, m - 2, (m - 1) // 2)))
    return k, idx


def feature_block(k, idx):
    return jnp.where(k == 3, (idx % 2) * 2 + idx // 2, jnp.where(k == 1, (idx + 2) % 4, idx))


def y_offset(k):
    return jnp.where(k == 2, 3, jnp.where(k == 3, 2, k))


def kernel(
    ids, acts, cotan, basis_in, basis_out, act_factor, grad_factor,
    precond, totals,
    cotb, actb, smp, own, cout, cin, zout, ra, rb, rcc, rd, xr, xst, wb, ts, tr, tb, fac, ebas, bout, eigb, eigs, scaled, right,
    lsem, y_ss, y_rs, x_ss, x_rs, c_ss, c_rs, z_ss, a_rs, b_rs, cc_rs, d_rs, xs_ss, xs_rs, w_ss, w_rs, t_ss, t_rs, tx_ss, tx_rs,
    tc_ss, tc_rs, e_ss, e_rs, ec_ss, ec_rs,
):
    r = lax.axis_index("dp")
    w = lax.axis_index("worker")
    z, xh, c = r // 4, (r // 2) % 2, r % 2
    y, xl = w // 2, w % 2
    x = xh * 2 + xl
    oc = 1 - c

    def at(dx=0, dy=0, dz=0):
        return device((x + dx) % NX, (y + dy) % NY, (z + dz) % NZ, c)

    core = device(x, y, z, oc)
    zp, zm, zp2, zm2 = at(dz=1), at(dz=7), at(dz=2), at(dz=6)
    yp, ym = at(dy=1), at(dy=3)
    far_x = (1 - xh) * 2 + xl
    part_x = xh * 2 + (1 - xl)
    cross_x = (1 - xh) * 2 + (1 - xl)
    partner = device(part_x, y, z, c)
    far = device(far_x, y, z, c)
    cross = device(cross_x, y, z, c)

    def rc(src, dst, ss, rs, dev):
        return pltpu.make_async_remote_copy(
            src_ref=src, dst_ref=dst, send_sem=ss, recv_sem=rs, device_id=dev, device_id_type=MESH
        )

    loads = []
    for q in range(4):
        into = cotb.at[q // 2, :, pl.ds((q % 2) * PIECE, PIECE)]
        loads.append(pltpu.make_async_copy(cotan.at[:, pl.ds(q * PIECE, PIECE)], into, lsem.at[q]))
    for h in range(2):
        loads.append(pltpu.make_async_copy(acts.at[:, pl.ds(h * HALF, HALF)], actb.at[xl, h], lsem.at[4 + h]))
    loads.append(pltpu.make_async_copy(basis_out.at[z], bout, lsem.at[6]))
    for cp in loads:
        cp.start()

    @pl.when(c == 0)
    def _():
        pltpu.make_async_copy(basis_in, ebas, lsem.at[7]).start()
        pltpu.make_async_copy(act_factor, fac, lsem.at[8]).start()

    @pl.when(c == 1)
    def _():
        pltpu.make_async_copy(basis_out.at[w], ebas, lsem.at[7]).start()
        pltpu.make_async_copy(grad_factor, fac, lsem.at[8]).start()

    barrier = pltpu.get_barrier_semaphore()
    for k in range(1, 8):
        wk = (w + k) % 8
        pl.semaphore_signal(barrier, inc=1, device_id=(r, wk), device_id_type=MESH)
    for dev in (core, zp, zm, zp2, zm2, far, cross):
        pl.semaphore_signal(barrier, inc=1, device_id=dev, device_id_type=MESH)
    pl.semaphore_wait(barrier, 14)

    def piece(n):
        return cotb.at[n // 2, :, pl.ds((n % 2) * PIECE, PIECE)]

    def send_p(k):
        n = (5, 7, 11, 15)[k]
        return rc(cotan.at[:, pl.ds(k * PIECE, PIECE)], piece(n), y_ss.at[k], y_rs.at[n], yp)

    def send_m(k):
        n = (4, 6, 10, 14)[k]
        q = (k + 2) % 4
        return rc(cotan.at[:, pl.ds(q * PIECE, PIECE)], piece(n), y_ss.at[4 + k], y_rs.at[n], ym)

    def fwd_p(k):
        src, dst = (5, 7)[k], (8, 12)[k]
        return rc(piece(src), piece(dst), y_ss.at[8 + k], y_rs.at[dst], yp)

    def fwd_m(k):
        src, dst = (4, 6)[k], (9, 13)[k]
        return rc(piece(src), piece(dst), y_ss.at[10 + k], y_rs.at[dst], ym)

    def send_x(h):
        return rc(acts.at[:, pl.ds(h * HALF, HALF)], actb.at[xl, h], x_ss.at[h], x_rs.at[h], partner)

    def recv_x(h):
        return rc(acts.at[:, pl.ds(h * HALF, HALF)], actb.at[1 - xl, h], x_ss.at[h], x_rs.at[h], partner)

    for k in range(2):
        send_p(k).start()
        send_m(k).start()
        send_x(k).start()

    def wait_piece(n):
        rc(piece(n), piece(n), y_ss.at[0], y_rs.at[n], yp).wait_recv()

    for cp in loads[:6]:
        cp.wait()

    def dist(i):
        k, _ = piece_source(kept_piece(unit_parts(i)[0], c))
        to = jnp.where(i < NF, i, 2 * ((y + y_offset(k)) % NY) + xl)
        return (to - z + NZ) % NZ

    def along(i, steps):
        return at(dz=jnp.where(i % 2 == 0, steps, NZ - steps))

    def core_copy(i):
        return rc(cout.at[i], cin.at[i], c_ss.at[i], c_rs.at[i], core)

    def z_copy(i, dev, land, sem):
        return rc(zout.at[i], land.at[i], z_ss.at[i], sem.at[i], dev)

    lands = {"a": (ra, a_rs), "b": (rb, b_rs), "c": (rcc, cc_rs), "d": (rd, d_rs)}

    def send_z(i, steps, slot):
        z_copy(i, along(i, steps), *lands[slot]).start()

    def recv_z(i, slots):
        for slot in slots:
            z_copy(i, zp, *lands[slot]).wait_recv()
        acc = own[i]
        for slot in slots:
            acc = acc + lands[slot][0][i].astype(F32)
        return acc.astype(BF)

    def compute_factor():
        scale_own = jnp.where(c == 0, 1.0 / 8192, 4.0).astype(F32)
        scale_other = jnp.where(c == 0, 4.0, 1.0 / 8192).astype(F32)
        for s in range(2):
            into = slice(s * BLK, (s + 1) * BLK)
            for h in range(2):
                block = actb[xl, h, :BLK, :]
                for k in range(1, 8):
                    block = jnp.where(ids[s] == k, actb[xl, h, k * BLK : (k + 1) * BLK, :], block)
                smp[0, into, h * HALF : (h + 1) * HALF] = block
            for q in range(4):
                cols = slice((q % 2) * PIECE, (q % 2 + 1) * PIECE)
                block = cotb[q // 2, :BLK, cols]
                for k in range(1, 8):
                    block = jnp.where(ids[s] == k, cotb[q // 2, k * BLK : (k + 1) * BLK, cols], block)
                smp[1, into, q * PIECE : (q + 1) * PIECE] = block

        @pl.loop(0, NF)
        def _(i):
            left = pl.ds(pl.multiple_of((i // 2) * PIECE, PIECE), PIECE)
            cols = pl.ds(pl.multiple_of((i % 2) * HALF, HALF), HALF)
            cout[i] = (tdot(smp[oc, :, left], smp[oc, :, cols]) * scale_other).astype(BF)
            core_copy(i).start()
            own[i] = tdot(smp[c, :, left], smp[c, :, cols]) * scale_own

    def compute(i):
        m, e, h = unit_parts(i)
        ea = jnp.where(e == 0, xl, 1 - xl)
        both = tdot(cotb[m], actb[ea, h])
        lower = kept_piece(m, c) % 2 == 0
        cout[i] = jnp.where(lower, both[PIECE:], both[:PIECE]).astype(BF)
        core_copy(i).start()
        own[i] = jnp.where(lower, both[:PIECE], both[PIECE:])

    def way(i):
        d = dist(i)
        return jnp.where(i % 2 == 0, d, (NZ - d) % NZ), i < NF, (i >= NF) & (i < SKIP_FROM), i >= SKIP_FROM

    def merge(i):
        core_copy(i).wait_recv()
        acc = own[i] + cin[i].astype(F32)
        own[i] = acc
        d, tree, chain, skip = way(i)
        near_up = (tree & ((d == 1) | (d == 3))) | (skip & (d == 3))
        near_down = tree & (d == 7)

        @pl.when((d == 4) | (d == 5) | near_up | near_down)
        def _():
            zout[i] = acc.astype(BF)

        @pl.when((d == 4) & tree)
        def _():
            send_z(i, 2, "a")

        @pl.when((d == 4) & skip)
        def _():
            send_z(i, 2, "c")

        @pl.when(((d == 4) & chain) | (tree & (d == 1)) | (skip & (d == 3)))
        def _():
            send_z(i, 1, "a")

        @pl.when(tree & (d == 3))
        def _():
            send_z(i, 1, "b")

        @pl.when((d == 5) | near_down)
        def _():
            send_z(i, 7, "b")

    def pass_on(i, cond, slots, steps, slot):
        @pl.when(cond)
        def _():
            zout[i] = recv_z(i, slots)
            send_z(i, steps, slot)

    def finish_z(i, cond, slots):
        @pl.when(cond)
        def _():
            total = recv_z(i, slots)

            @pl.when(i < NF)
            def _():
                ts[...] = total
                rc(ts, tr, tx_ss.at[0], tx_rs.at[0], far).start()

            @pl.when(i >= NF)
            def _():
                m, e, h = unit_parts(i)
                q = feature_block(*piece_source(kept_piece(m, c)))

                @pl.when(e == 0)
                def _():
                    xr[xh, q, h] = total
                    rc(xr.at[xh, q, h], xr.at[xh, q, h], xs_ss.at[0, q, h], xs_rs.at[xh, q, h], far).start()

                @pl.when(e == 1)
                def _():
                    xst[q, h] = total
                    rc(xst.at[q, h], xr.at[xh, q, h], xs_ss.at[1, q, h], xs_rs.at[xh, q, h], partner).start()
                    rc(xst.at[q, h], xr.at[xh, q, h], xs_ss.at[2, q, h], xs_rs.at[xh, q, h], cross).start()

    def hop_1(i):
        d, tree, chain, skip = way(i)
        pass_on(i, (d == 3) & chain, "a", 1, "a")
        pass_on(i, (d == 2) & skip, "ac", 1, "a")
        pass_on(i, (d == 6) & (chain | skip), "b", 7, "b")
        pass_on(i, (d == 2) & tree, "ab", 2, "c")
        pass_on(i, (d == 6) & tree, "b", 6, "d")

    def hop_2(i):
        d, tree, chain, skip = way(i)
        pass_on(i, ((d == 2) & chain) | ((d == 1) & skip), "a", 1, "a")
        pass_on(i, (d == 7) & (chain | skip), "b", 7, "b")
        finish_z(i, (d == 0) & tree, "abcd")

    def hop_3(i):
        d, _, chain, skip = way(i)
        pass_on(i, (d == 1) & chain, "a", 1, "a")
        finish_z(i, (d == 0) & skip, "ab")

    def hop_4(i):
        d, _, chain, _ = way(i)
        finish_z(i, (d == 0) & chain, "ab")

    stages = (compute, merge, hop_1, hop_2, hop_3, hop_4)
    done = [NF] * len(stages)

    def advance(stage, to):
        lo, to = done[stage], min(to, NU)
        if to > lo:
            pl.loop(lo, to)(stages[stage])
            done[stage] = to

    def advance_all(to, lags):
        for stage in range(len(stages) - 1, 0, -1):
            advance(stage, to - lags[stage])

    def run(to, lags):
        lo = done[0]
        advance_all(lo, lags)

        @pl.loop(lo, to)
        def _(i):
            compute(i)
            for stage in range(1, len(stages)):
                first, lag = done[stage], lags[stage]
                if to - lag > first:
                    if lo - lag >= first:
                        stages[stage](i - lag)
                    else:
                        pl.when(i - lag >= first)(lambda stage=stage, lag=lag: stages[stage](i - lag))

        done[0] = to
        for stage in range(1, len(stages)):
            done[stage] = max(done[stage], to - lags[stage])

    def each_factor(step):
        pl.loop(0, NF)(step)

    def t_copy(o, k, dev):
        return rc(tb.at[c, o], tb.at[c, o], t_ss.at[k], t_rs.at[o], dev)

    def t_core(o):
        return rc(tb.at[c, o], tb.at[c, o], tc_ss.at[o], tc_rs.at[o], core)

    def t_core_recv(o):
        return rc(tb.at[oc, o], tb.at[oc, o], tc_ss.at[o], tc_rs.at[o], core)

    def origin(dz):
        return (z + dz) % NZ

    def spread_1():
        rc(ts, tr, tx_ss.at[0], tx_rs.at[0], far).wait_recv()
        tb[c, z] = (ts[...].astype(F32) + tr[...].astype(F32)).astype(BF)
        for k, dev in enumerate((zp, zm, zp2, zm2)):
            t_copy(z, k, dev).start()
        t_core(z).start()

    def t_arrived(dz):
        o = origin(dz)
        t_copy(o, 0, zp).wait_recv()
        t_core(o).start()

    def spread_2():
        back, ahead = jnp.where(c == 0, 6, 2), jnp.where(c == 0, 2, 6)
        t_arrived(back)
        t_copy(origin(back), 4, along(c, 1)).start()
        t_copy(origin(back), 5, along(c, 2)).start()
        t_arrived(ahead)
        t_copy(origin(ahead), 6, along(c, 7)).start()
        t_arrived(7)
        t_arrived(1)

    def spread_3():
        t_arrived(5)
        t_arrived(3)
        t_arrived(4)

    def eigen_chunks(lo, hi):
        if lo == 6:
            pltpu.make_async_copy(act_factor, fac, lsem.at[8]).wait()
            pltpu.make_async_copy(basis_in, ebas, lsem.at[7]).wait()
            eigs[...] = jnp.zeros_like(eigs)

        @pl.loop(lo, hi)
        def _(dz):
            o = (z + dz) % NZ
            rows = pl.ds(pl.multiple_of((o // 2) * PIECE, PIECE), PIECE)
            cols = pl.ds(pl.multiple_of((o % 2) * HALF, HALF), HALF)
            new = DECAY_RATE * fac[rows, cols] + (1.0 - DECAY_RATE) * tb[c, o].astype(F32)
            basis = ebas[cols, :]
            prod = jnp.zeros((PIECE, FB), F32)
            for _ in range(3):
                part = new.astype(BF)
                prod = prod + ndot(part, basis)
                new = new - part.astype(F32)
            prod = prod * ebas[rows, :].astype(F32)
            eigs[...] += jnp.sum(prod.reshape(PIECE // 8, 8, FB), axis=0)

    def total_copy(f, o):
        into = totals.at[f, pl.ds((o // 2) * PIECE, PIECE), pl.ds((o % 2) * HALF, HALF)]
        return pltpu.make_async_copy(tb.at[f, o], into, lsem.at[10 + f * NF + o])

    def factor_outputs():
        for o in range(NF):
            t_core_recv(o).wait_recv()
        for f in range(2):
            for o in range(NF):
                total_copy(f, o).start()

    def eigen_end():
        eig = jnp.broadcast_to(jnp.sum(eigs[...], axis=0, keepdims=True), (8, FB))

        @pl.when(c == 0)
        def _():
            eigb[0] = eig
            rc(eigb.at[0], eigb.at[0], ec_ss, ec_rs, core).start()

        @pl.when((c == 1) & (w == z))
        def _():
            eigb[1] = eig
            for k in range(1, 8):
                rc(eigb.at[1], eigb.at[1], e_ss.at[k - 1], e_rs, (r, (w + k) % 8)).start()

    def eigen_pass():
        @pl.when(c == 1)
        def _():
            @pl.when(w != z)
            def _():
                rc(eigb.at[1], eigb.at[1], e_ss.at[0], e_rs, (r, z)).wait_recv()

            rc(eigb.at[1], eigb.at[1], ec_ss, ec_rs, core).start()

    lags = (0, 2, 7, 12, 17, 22)
    compute_factor()
    each_factor(merge)
    run(12, lags)
    advance(1, 12)
    each_factor(hop_1)
    wait_piece(5)
    fwd_p(0).start()
    send_p(2).start()
    wait_piece(4)
    fwd_m(0).start()
    send_m(2).start()
    run(14, lags)
    advance(1, 14)
    advance(2, 12)
    each_factor(hop_2)
    wait_piece(7)
    fwd_p(1).start()
    send_p(3).start()
    wait_piece(6)
    fwd_m(1).start()
    send_m(3).start()
    run(16, lags)
    recv_x(0).wait_recv()
    run(20, lags)
    advance(1, 20)
    advance(3, 12)
    advance(2, 14)
    spread_1()
    wait_piece(8)
    wait_piece(9)
    run(23, lags)
    advance(1, 23)
    advance(4, 12)
    advance(3, 14)
    advance(2, 20)
    spread_2()
    eigen_chunks(6, 11)
    wait_piece(10)
    wait_piece(11)
    run(26, lags)
    recv_x(1).wait_recv()
    run(32, lags)
    spread_3()
    wait_piece(12)
    wait_piece(13)
    run(36, lags)
    wait_piece(14)
    wait_piece(15)
    run(40, lags)
    advance(1, 40)
    eigen_chunks(3, 6)
    eigen_end()
    for to in range(41, 53):
        advance_all(to, lags)
    factor_outputs()
    for to in range(53, 40 + 23):
        advance_all(to, lags)
    eigen_pass()

    pltpu.make_async_copy(basis_out.at[z], bout, lsem.at[6]).wait()
    def w_copy(q):
        return rc(wb.at[q], wb.at[q], w_ss.at[q], w_rs.at[q], core)

    home = (z % 2) == xl
    dy = (z // 2 - y + NY) % NY
    shard = jnp.where(dy == 3, 2, jnp.where(dy == 2, 3, dy))

    def mine_first(idx):
        return jnp.where(shard == 2, 1 - idx % 2, idx % 2) == c

    @pl.loop(0, 4)
    def _(idx):
        q = feature_block(shard, idx)

        @pl.when(mine_first(idx))
        def _():
            for h in range(2):
                @pl.when(jnp.logical_not(home))
                def _():
                    rc(xst.at[q, h], xr.at[xh, q, h], xs_ss.at[0, q, h], xs_rs.at[xh, q, h], far).wait_recv()

                rc(xst.at[q, h], xr.at[1 - xh, q, h], xs_ss.at[0, q, h], xs_rs.at[1 - xh, q, h], far).wait_recv()
                wb[q, :, h * HALF : (h + 1) * HALF] = (
                    xr[0, q, h].astype(F32) + xr[1, q, h].astype(F32)
                ).astype(BF)
            w_copy(q).start()

    @pl.loop(0, 4)
    def _(idx):
        q = feature_block(shard, idx)

        @pl.when(jnp.logical_not(mine_first(idx)))
        def _():
            w_copy(q).wait_recv()

        rows = pl.ds(pl.multiple_of(q * PIECE, PIECE), PIECE)
        right[rows, :] = ndot(wb[q], basis_in[...]).astype(BF)

    @pl.when(c == 0)
    def _():
        rc(eigb.at[1], eigb.at[1], ec_ss, ec_rs, core).wait_recv()

    @pl.when(c == 1)
    def _():
        rc(eigb.at[0], eigb.at[0], ec_ss, ec_rs, core).wait_recv()

    ei = eigb[0, 0:1, :]
    for a in range(4):
        rows = slice(a * PIECE, (a + 1) * PIECE)
        eo = jnp.transpose(jnp.broadcast_to(eigb[1, 0:1, rows], (PIECE, PIECE)))
        eo = jnp.concatenate([eo] * 4, axis=1)
        scaled[rows, :] = (tdot(bout[:, rows], right[...]) / (eo * ei + DAMPING)).astype(BF)
    mine = pl.ds(pl.multiple_of((xh * 2 + c) * PIECE, PIECE), PIECE)
    upper = ndot(bout[mine, :], scaled[...]).astype(BF)
    precond[...] = lax.dot_general(
        upper, basis_in[...], (((1,), (1,)), ((), ())), preferred_element_type=F32
    ).astype(BF)

    for k in range(4):
        send_p(k).wait_send()
        send_m(k).wait_send()
    for k in range(2):
        fwd_p(k).wait_send()
        fwd_m(k).wait_send()
        send_x(k).wait_send()

    @pl.loop(0, NU)
    def _(i):
        core_copy(i).wait_send()

        @pl.when(dist(i) != 0)
        def _():
            z_copy(i, zp, ra, a_rs).wait_send()

    rc(ts, tr, tx_ss.at[0], tx_rs.at[0], far).wait_send()
    for k in range(7):
        t_copy(z, k, zp).wait_send()
    for o in range(NF):
        t_core(o).wait_send()

    @pl.when(home)
    def _():
        @pl.loop(0, 4)
        def _(idx):
            q = feature_block(shard, idx)

            @pl.when(mine_first(idx))
            def _():
                for k in range(3):
                    for h in range(2):
                        rc(
                            xst.at[q, h], xr.at[xh, q, h], xs_ss.at[k, q, h], xs_rs.at[xh, q, h], far
                        ).wait_send()

    @pl.loop(0, 4)
    def _(idx):
        @pl.when(mine_first(idx))
        def _():
            w_copy(feature_block(shard, idx)).wait_send()

    rc(eigb.at[0], eigb.at[0], ec_ss, ec_rs, core).wait_send()

    @pl.when((c == 1) & (w == z))
    def _():
        for k in range(1, 8):
            rc(eigb.at[1], eigb.at[1], e_ss.at[k - 1], e_rs, (r, (w + k) % 8)).wait_send()

    for f in range(2):
        for o in range(NF):
            total_copy(f, o).wait()


def update(precond, totals, act_factor, grad_factor, precond_out, act_new, grad_new):
    precond_out[...] = precond[...]
    act_new[0] = DECAY_RATE * act_factor[0] + (1.0 - DECAY_RATE) * totals[0].astype(F32)
    grad_new[0] = DECAY_RATE * grad_factor[0] + (1.0 - DECAY_RATE) * totals[1].astype(F32)


def per_device(acts, cotan, block_ids, basis_in, basis_out, act_factor, grad_factor):
    vm = pltpu.VMEM
    dma = pltpu.SemaphoreType.DMA
    unit = (PIECE, HALF)
    any_spec = pl.BlockSpec(memory_space=pltpu.HBM)
    precond, totals = pl.pallas_call(
        kernel,
        name="kfac",
        out_shape=(
            jax.ShapeDtypeStruct((PIECE, FB), BF),
            jax.ShapeDtypeStruct((2, FB, FB), BF),
        ),
        in_specs=[
            pl.BlockSpec(memory_space=pltpu.SMEM),
            any_spec,
            any_spec,
            pl.BlockSpec(memory_space=pltpu.VMEM),
            any_spec,
            any_spec,
            any_spec,
        ],
        out_specs=(pl.BlockSpec(memory_space=pltpu.VMEM),) * 2,
        scratch_shapes=[
            vm((8, 1024, HALF), BF),
            vm((2, 2, 1024, HALF), BF),
            vm((2, 2 * BLK, FB), BF),
            vm((NU,) + unit, F32),
            vm((NU,) + unit, BF),
            vm((NU,) + unit, BF),
            vm((NU,) + unit, BF),
            vm((NU,) + unit, BF),
            vm((NU,) + unit, BF),
            vm((NU,) + unit, BF),
            vm((NU,) + unit, BF),
            vm((2, 4, 2) + unit, BF),
            vm((4, 2) + unit, BF),
            vm((4, PIECE, FB), BF),
            vm(unit, BF),
            vm(unit, BF),
            vm((2, NF) + unit, BF),
            vm((FB, FB), F32),
            vm((FB, FB), BF),
            vm((FB, FB), BF),
            vm((2, 8, FB), F32),
            vm((8, FB), F32),
            vm((FB, FB), BF),
            vm((FB, FB), BF),
            dma((26,)),
            dma((12,)),
            dma((16,)),
            dma((2,)),
            dma((2,)),
            dma((NU,)),
            dma((NU,)),
            dma((NU,)),
            dma((NU,)),
            dma((NU,)),
            dma((NU,)),
            dma((NU,)),
            dma((3, 4, 2)),
            dma((2, 4, 2)),
            dma((4,)),
            dma((4,)),
            dma((7,)),
            dma((NF,)),
            dma((1,)),
            dma((1,)),
            dma((NF,)),
            dma((NF,)),
            dma((7,)),
            dma,
            dma,
            dma,
        ],
        compiler_params=pltpu.CompilerParams(
            collective_id=0, has_side_effects=True, vmem_limit_bytes=60 << 20
        ),
    )(
        block_ids,
        acts,
        cotan,
        basis_in.reshape(FB, FB),
        basis_out,
        act_factor.reshape(FB, FB),
        grad_factor.reshape(FB, FB),
    )
    steps = 4
    rows = pl.BlockSpec((PIECE // steps, FB), lambda i: (i, 0))
    both = pl.BlockSpec((2, FB // steps, FB), lambda i: (0, i, 0))
    factor = pl.BlockSpec((1, FB // steps, FB), lambda i: (0, i, 0))
    return pl.pallas_call(
        update,
        name="update",
        grid=(steps,),
        in_specs=[rows, both, factor, factor],
        out_specs=(rows, factor, factor),
        out_shape=(
            jax.ShapeDtypeStruct((PIECE, FB), BF),
            jax.ShapeDtypeStruct((1, FB, FB), F32),
            jax.ShapeDtypeStruct((1, FB, FB), F32),
        ),
        compiler_params=pltpu.CompilerParams(vmem_limit_bytes=60 << 20),
    )(precond, totals, act_factor, grad_factor)


def solution(mesh):
    return jax.shard_map(
        per_device,
        mesh=mesh,
        in_specs=(
            P("dp", "worker"),
            P("dp", "worker"),
            P("dp"),
            P("worker", None, None),
            P(),
            P("worker", None, None),
            P("worker", None, None),
        ),
        out_specs=(P("dp", "worker"), P("worker", None, None), P("worker", None, None)),
        check_vma=False,
    )
```

```python
import jax
import jax.numpy as jnp
from jax import lax
from jax.experimental import pallas as pl
from jax.experimental.pallas import tpu as pltpu
from jax.sharding import PartitionSpec as P

MESH = pl.DeviceIdType.MESH
DECAY_RATE = 0.75
DAMPING = 0.03
BLK = 128
NX, NY, NZ = 4, 4, 8
FB = 512
PIECE = 128
HALF = 256
NF = 8
NU = 40
SKIP_FROM = 36
BF = jnp.bfloat16
F32 = jnp.float32


def tdot(a, b):
    return lax.dot_general(a, b, (((0,), (0,)), ((), ())), preferred_element_type=F32)


def ndot(a, b):
    return lax.dot_general(a, b, (((1,), (0,)), ((), ())), preferred_element_type=F32)


def device(x, y, z, c):
    return (z * 4 + (x // 2) * 2 + c, y * 2 + x % 2)


def weight_units():
    units = [(m, 0, h) for m in range(4) for h in range(2)]
    units += [(m, 1, 0) for m in range(4)]
    for m in (4, 5):
        units += [(m, 0, 0), (m, 0, 1), (m, 1, 0)]
    units += [(m, 1, 1) for m in range(6)]
    return units + [(m, e, h) for m in (6, 7) for e in range(2) for h in range(2)]


def packed(values, bits):
    word = sum(v << (bits * k) for k, v in enumerate(values))
    return word - (1 << 32) if word >= 1 << 31 else word


def field(word, place, bits):
    return lax.shift_right_logical(word, jnp.int32(bits) * place) & ((1 << bits) - 1)


PAIR_ACTS = [packed([2 * m + e for m, e, _ in weight_units()[g : g + 8]], 4) for g in range(0, 32, 8)]
PART = packed([h for _, _, h in weight_units()], 1)


def shard_offset(m, c):
    side = 1 - c if m in (3, 7) else c
    return 0 if m < 2 else 2 if m in (4, 6) else 3 if side else 1


OFFSETS = [
    [packed([shard_offset(m, c) for m, _, _ in weight_units()[g : g + 16]], 2) for g in (0, 16)] for c in range(2)
]


def unit_parts(i):
    j = i - NF
    group = j >> 3
    word = jnp.int32(PAIR_ACTS[0])
    for g in range(1, 4):
        word = jnp.where(group == g, jnp.int32(PAIR_ACTS[g]), word)
    both = field(word, j & 7, 4)
    return both >> 1, both & 1, field(jnp.int32(PART), j, 1)


def kept_piece(m, c):
    return 2 * m + jnp.where((m == 3) | (m == 7), 1 - c, c)


def piece_source(n):
    m = n // 2
    far = (m == 4) | (m == 6)
    k = jnp.where(m < 2, 0, jnp.where(far, 3, 1 + n % 2))
    far_idx = jnp.where(m == 6, 2, 0) + n % 2
    idx = jnp.where(m < 2, n, jnp.where(far, far_idx, jnp.where(m < 4, m - 2, (m - 1) // 2)))
    return k, idx


def feature_block(k, idx):
    return jnp.where(k == 3, (idx % 2) * 2 + idx // 2, jnp.where(k == 1, (idx + 2) % 4, idx))


def y_offset(k):
    return jnp.where(k == 2, 3, jnp.where(k == 3, 2, k))


def kernel(
    ids, acts, cotan, basis_in, basis_out, act_factor, grad_factor,
    precond, totals,
    cotb, actb, smp, own, cout, cin, zout, ra, rb, rcc, rd, xr, xst, wb, ts, tr, tb, fac, ebas, bout, eigb, eigs, scaled, right,
    lsem, y_ss, y_rs, x_ss, x_rs, c_ss, c_rs, z_ss, a_rs, b_rs, cc_rs, d_rs, xs_ss, xs_rs, w_ss, w_rs, t_ss, t_rs, tx_ss, tx_rs,
    tc_ss, tc_rs, e_ss, e_rs, ec_ss, ec_rs,
):
    r = lax.axis_index("dp")
    w = lax.axis_index("worker")
    z, xh, c = r // 4, (r // 2) % 2, r % 2
    y, xl = w // 2, w % 2
    x = xh * 2 + xl
    oc = 1 - c

    def at(dx=0, dy=0, dz=0):
        return device((x + dx) % NX, (y + dy) % NY, (z + dz) % NZ, c)

    core = device(x, y, z, oc)
    zp, zm, zp2, zm2 = at(dz=1), at(dz=7), at(dz=2), at(dz=6)
    yp, ym = at(dy=1), at(dy=3)
    far_x = (1 - xh) * 2 + xl
    part_x = xh * 2 + (1 - xl)
    cross_x = (1 - xh) * 2 + (1 - xl)
    partner = device(part_x, y, z, c)
    far = device(far_x, y, z, c)
    cross = device(cross_x, y, z, c)

    def rc(src, dst, ss, rs, dev):
        return pltpu.make_async_remote_copy(
            src_ref=src, dst_ref=dst, send_sem=ss, recv_sem=rs, device_id=dev, device_id_type=MESH
        )

    loads = []
    for q in range(4):
        into = cotb.at[q // 2, :, pl.ds((q % 2) * PIECE, PIECE)]
        loads.append(pltpu.make_async_copy(cotan.at[:, pl.ds(q * PIECE, PIECE)], into, lsem.at[q]))
    for h in range(2):
        loads.append(pltpu.make_async_copy(acts.at[:, pl.ds(h * HALF, HALF)], actb.at[xl, h], lsem.at[4 + h]))
    loads.append(pltpu.make_async_copy(basis_out.at[z], bout, lsem.at[6]))
    for cp in loads:
        cp.start()

    @pl.when(c == 0)
    def _():
        pltpu.make_async_copy(basis_in, ebas, lsem.at[7]).start()
        pltpu.make_async_copy(act_factor, fac, lsem.at[8]).start()

    @pl.when(c == 1)
    def _():
        pltpu.make_async_copy(basis_out.at[w], ebas, lsem.at[7]).start()
        pltpu.make_async_copy(grad_factor, fac, lsem.at[8]).start()

    barrier = pltpu.get_barrier_semaphore()
    for k in range(1, 8):
        wk = (w + k) % 8
        pl.semaphore_signal(barrier, inc=1, device_id=(r, wk), device_id_type=MESH)
    for dev in (core, zp, zm, zp2, zm2, far, cross):
        pl.semaphore_signal(barrier, inc=1, device_id=dev, device_id_type=MESH)
    pl.semaphore_wait(barrier, 14)

    def piece(n):
        return cotb.at[n // 2, :, pl.ds((n % 2) * PIECE, PIECE)]

    def send_p(k):
        n = (5, 7, 11, 15)[k]
        return rc(cotan.at[:, pl.ds(k * PIECE, PIECE)], piece(n), y_ss.at[k], y_rs.at[n], yp)

    def send_m(k):
        n = (4, 6, 10, 14)[k]
        q = (k + 2) % 4
        return rc(cotan.at[:, pl.ds(q * PIECE, PIECE)], piece(n), y_ss.at[4 + k], y_rs.at[n], ym)

    def fwd_p(k):
        src, dst = (5, 7)[k], (8, 12)[k]
        return rc(piece(src), piece(dst), y_ss.at[8 + k], y_rs.at[dst], yp)

    def fwd_m(k):
        src, dst = (4, 6)[k], (9, 13)[k]
        return rc(piece(src), piece(dst), y_ss.at[10 + k], y_rs.at[dst], ym)

    def send_x(h):
        return rc(acts.at[:, pl.ds(h * HALF, HALF)], actb.at[xl, h], x_ss.at[h], x_rs.at[h], partner)

    def recv_x(h):
        return rc(acts.at[:, pl.ds(h * HALF, HALF)], actb.at[1 - xl, h], x_ss.at[h], x_rs.at[h], partner)

    for k in range(2):
        send_p(k).start()
        send_m(k).start()
        send_x(k).start()

    def wait_piece(n):
        rc(piece(n), piece(n), y_ss.at[0], y_rs.at[n], yp).wait_recv()

    for cp in loads[:6]:
        cp.wait()

    offsets = [jnp.where(c == 0, jnp.int32(OFFSETS[0][g]), jnp.int32(OFFSETS[1][g])) for g in range(2)]

    def dist(i):
        j = i - NF
        dy = field(jnp.where(j < 16, offsets[0], offsets[1]), j & 15, 2)
        to = jnp.where(i < NF, i, 2 * ((y + dy) & (NY - 1)) + xl)
        return (to - z + NZ) & (NZ - 1)

    def along(i, steps):
        return at(dz=jnp.where(i % 2 == 0, steps, NZ - steps))

    def core_copy(i):
        return rc(cout.at[i], cin.at[i], c_ss.at[i], c_rs.at[i], core)

    def z_copy(i, dev, land, sem):
        return rc(zout.at[i], land.at[i], z_ss.at[i], sem.at[i], dev)

    lands = {"a": (ra, a_rs), "b": (rb, b_rs), "c": (rcc, cc_rs), "d": (rd, d_rs)}

    def send_z(i, steps, slot):
        z_copy(i, along(i, steps), *lands[slot]).start()

    def recv_z(i, slots):
        for slot in slots:
            z_copy(i, zp, *lands[slot]).wait_recv()
        acc = own[i]
        for slot in slots:
            acc = acc + lands[slot][0][i].astype(F32)
        return acc.astype(BF)

    def compute_factor():
        scale_own = jnp.where(c == 0, 1.0 / 8192, 4.0).astype(F32)
        scale_other = jnp.where(c == 0, 4.0, 1.0 / 8192).astype(F32)
        for s in range(2):
            into = slice(s * BLK, (s + 1) * BLK)
            for h in range(2):
                block = actb[xl, h, :BLK, :]
                for k in range(1, 8):
                    block = jnp.where(ids[s] == k, actb[xl, h, k * BLK : (k + 1) * BLK, :], block)
                smp[0, into, h * HALF : (h + 1) * HALF] = block
            for q in range(4):
                cols = slice((q % 2) * PIECE, (q % 2 + 1) * PIECE)
                block = cotb[q // 2, :BLK, cols]
                for k in range(1, 8):
                    block = jnp.where(ids[s] == k, cotb[q // 2, k * BLK : (k + 1) * BLK, cols], block)
                smp[1, into, q * PIECE : (q + 1) * PIECE] = block

        @pl.loop(0, NF)
        def _(i):
            left = pl.ds(pl.multiple_of((i // 2) * PIECE, PIECE), PIECE)
            cols = pl.ds(pl.multiple_of((i % 2) * HALF, HALF), HALF)
            cout[i] = (tdot(smp[oc, :, left], smp[oc, :, cols]) * scale_other).astype(BF)
            core_copy(i).start()
            own[i] = tdot(smp[c, :, left], smp[c, :, cols]) * scale_own

    def compute(i):
        m, e, h = unit_parts(i)
        ea = jnp.where(e == 0, xl, 1 - xl)
        both = tdot(cotb[m], actb[ea, h])
        lower = kept_piece(m, c) % 2 == 0
        cout[i] = jnp.where(lower, both[PIECE:], both[:PIECE]).astype(BF)
        core_copy(i).start()
        own[i] = jnp.where(lower, both[:PIECE], both[PIECE:])

    def way(i):
        d = dist(i)
        return jnp.where(i % 2 == 0, d, (NZ - d) % NZ), i < NF, (i >= NF) & (i < SKIP_FROM), i >= SKIP_FROM

    def merge(i):
        core_copy(i).wait_recv()
        acc = own[i] + cin[i].astype(F32)
        own[i] = acc
        d, tree, chain, skip = way(i)
        near_up = (tree & ((d == 1) | (d == 3))) | (skip & (d == 3))
        near_down = tree & (d == 7)

        @pl.when((d == 4) | (d == 5) | near_up | near_down)
        def _():
            zout[i] = acc.astype(BF)

        @pl.when((d == 4) & tree)
        def _():
            send_z(i, 2, "a")

        @pl.when((d == 4) & skip)
        def _():
            send_z(i, 2, "c")

        @pl.when(((d == 4) & chain) | (tree & (d == 1)) | (skip & (d == 3)))
        def _():
            send_z(i, 1, "a")

        @pl.when(tree & (d == 3))
        def _():
            send_z(i, 1, "b")

        @pl.when((d == 5) | near_down)
        def _():
            send_z(i, 7, "b")

    def pass_on(i, cond, slots, steps, slot):
        @pl.when(cond)
        def _():
            zout[i] = recv_z(i, slots)
            send_z(i, steps, slot)

    def finish_z(i, cond, slots):
        @pl.when(cond)
        def _():
            total = recv_z(i, slots)

            @pl.when(i < NF)
            def _():
                ts[...] = total
                rc(ts, tr, tx_ss.at[0], tx_rs.at[0], far).start()

            @pl.when(i >= NF)
            def _():
                m, e, h = unit_parts(i)
                q = feature_block(*piece_source(kept_piece(m, c)))

                @pl.when(e == 0)
                def _():
                    xr[xh, q, h] = total
                    rc(xr.at[xh, q, h], xr.at[xh, q, h], xs_ss.at[0, q, h], xs_rs.at[xh, q, h], far).start()

                @pl.when(e == 1)
                def _():
                    xst[q, h] = total
                    rc(xst.at[q, h], xr.at[xh, q, h], xs_ss.at[1, q, h], xs_rs.at[xh, q, h], partner).start()
                    rc(xst.at[q, h], xr.at[xh, q, h], xs_ss.at[2, q, h], xs_rs.at[xh, q, h], cross).start()

    def hop_1(i):
        d, tree, chain, skip = way(i)
        pass_on(i, (d == 3) & chain, "a", 1, "a")
        pass_on(i, (d == 2) & skip, "ac", 1, "a")
        pass_on(i, (d == 6) & (chain | skip), "b", 7, "b")
        pass_on(i, (d == 2) & tree, "ab", 2, "c")
        pass_on(i, (d == 6) & tree, "b", 6, "d")

    def hop_2(i):
        d, tree, chain, skip = way(i)
        pass_on(i, ((d == 2) & chain) | ((d == 1) & skip), "a", 1, "a")
        pass_on(i, (d == 7) & (chain | skip), "b", 7, "b")
        finish_z(i, (d == 0) & tree, "abcd")

    def hop_3(i):
        d, _, chain, skip = way(i)
        pass_on(i, (d == 1) & chain, "a", 1, "a")
        finish_z(i, (d == 0) & skip, "ab")

    def hop_4(i):
        d, _, chain, _ = way(i)
        finish_z(i, (d == 0) & chain, "ab")

    stages = (compute, merge, hop_1, hop_2, hop_3, hop_4)
    done = [NF] * len(stages)

    def advance(stage, to):
        lo, to = done[stage], min(to, NU)
        if to > lo:
            pl.loop(lo, to)(stages[stage])
            done[stage] = to

    def advance_all(to, lags):
        for stage in range(len(stages) - 1, 0, -1):
            advance(stage, to - lags[stage])

    def run(to, lags):
        lo = done[0]
        advance_all(lo, lags)

        @pl.loop(lo, to)
        def _(i):
            compute(i)
            for stage in range(1, len(stages)):
                first, lag = done[stage], lags[stage]
                if to - lag > first:
                    if lo - lag >= first:
                        stages[stage](i - lag)
                    else:
                        pl.when(i - lag >= first)(lambda stage=stage, lag=lag: stages[stage](i - lag))

        done[0] = to
        for stage in range(1, len(stages)):
            done[stage] = max(done[stage], to - lags[stage])

    def each_factor(step):
        pl.loop(0, NF)(step)

    def t_copy(o, k, dev):
        return rc(tb.at[c, o], tb.at[c, o], t_ss.at[k], t_rs.at[o], dev)

    def t_core(o):
        return rc(tb.at[c, o], tb.at[c, o], tc_ss.at[o], tc_rs.at[o], core)

    def t_core_recv(o):
        return rc(tb.at[oc, o], tb.at[oc, o], tc_ss.at[o], tc_rs.at[o], core)

    def origin(dz):
        return (z + dz) % NZ

    def spread_1():
        rc(ts, tr, tx_ss.at[0], tx_rs.at[0], far).wait_recv()
        tb[c, z] = (ts[...].astype(F32) + tr[...].astype(F32)).astype(BF)
        for k, dev in enumerate((zp, zm, zp2, zm2)):
            t_copy(z, k, dev).start()
        t_core(z).start()

    def t_arrived(dz):
        o = origin(dz)
        t_copy(o, 0, zp).wait_recv()
        t_core(o).start()

    def spread_2():
        back, ahead = jnp.where(c == 0, 6, 2), jnp.where(c == 0, 2, 6)
        t_arrived(back)
        t_copy(origin(back), 4, along(c, 1)).start()
        t_copy(origin(back), 5, along(c, 2)).start()
        t_arrived(ahead)
        t_copy(origin(ahead), 6, along(c, 7)).start()
        t_arrived(7)
        t_arrived(1)

    def spread_3():
        t_arrived(5)
        t_arrived(3)
        t_arrived(4)

    def eigen_chunks(lo, hi):
        if lo == 6:
            pltpu.make_async_copy(act_factor, fac, lsem.at[8]).wait()
            pltpu.make_async_copy(basis_in, ebas, lsem.at[7]).wait()
            eigs[...] = jnp.zeros_like(eigs)

        @pl.loop(lo, hi)
        def _(dz):
            o = (z + dz) % NZ
            rows = pl.ds(pl.multiple_of((o // 2) * PIECE, PIECE), PIECE)
            cols = pl.ds(pl.multiple_of((o % 2) * HALF, HALF), HALF)
            new = DECAY_RATE * fac[rows, cols] + (1.0 - DECAY_RATE) * tb[c, o].astype(F32)
            basis = ebas[cols, :]
            prod = jnp.zeros((PIECE, FB), F32)
            for _ in range(3):
                part = new.astype(BF)
                prod = prod + ndot(part, basis)
                new = new - part.astype(F32)
            prod = prod * ebas[rows, :].astype(F32)
            eigs[...] += jnp.sum(prod.reshape(PIECE // 8, 8, FB), axis=0)

    def total_copy(f, o):
        into = totals.at[f, pl.ds((o // 2) * PIECE, PIECE), pl.ds((o % 2) * HALF, HALF)]
        return pltpu.make_async_copy(tb.at[f, o], into, lsem.at[10 + f * NF + o])

    def factor_outputs():
        for o in range(NF):
            t_core_recv(o).wait_recv()
        for f in range(2):
            for o in range(NF):
                total_copy(f, o).start()

    def eigen_end():
        eig = jnp.broadcast_to(jnp.sum(eigs[...], axis=0, keepdims=True), (8, FB))

        @pl.when(c == 0)
        def _():
            eigb[0] = eig
            rc(eigb.at[0], eigb.at[0], ec_ss, ec_rs, core).start()

        @pl.when((c == 1) & (w == z))
        def _():
            eigb[1] = eig
            for k in range(1, 8):
                rc(eigb.at[1], eigb.at[1], e_ss.at[k - 1], e_rs, (r, (w + k) % 8)).start()

    def eigen_pass():
        @pl.when(c == 1)
        def _():
            @pl.when(w != z)
            def _():
                rc(eigb.at[1], eigb.at[1], e_ss.at[0], e_rs, (r, z)).wait_recv()

            rc(eigb.at[1], eigb.at[1], ec_ss, ec_rs, core).start()

    lags = (0, 2, 7, 12, 17, 22)
    compute_factor()
    each_factor(merge)
    run(12, lags)
    advance(1, 12)
    each_factor(hop_1)
    wait_piece(5)
    fwd_p(0).start()
    send_p(2).start()
    wait_piece(4)
    fwd_m(0).start()
    send_m(2).start()
    run(14, lags)
    advance(1, 14)
    advance(2, 12)
    each_factor(hop_2)
    wait_piece(7)
    fwd_p(1).start()
    send_p(3).start()
    wait_piece(6)
    fwd_m(1).start()
    send_m(3).start()
    run(16, lags)
    recv_x(0).wait_recv()
    run(20, lags)
    advance(1, 20)
    advance(3, 12)
    advance(2, 14)
    spread_1()
    wait_piece(8)
    wait_piece(9)
    run(23, lags)
    advance(1, 23)
    advance(4, 12)
    advance(3, 14)
    advance(2, 20)
    spread_2()
    eigen_chunks(6, 11)
    wait_piece(10)
    wait_piece(11)
    run(26, lags)
    recv_x(1).wait_recv()
    run(32, lags)
    spread_3()
    wait_piece(12)
    wait_piece(13)
    run(36, lags)
    wait_piece(14)
    wait_piece(15)
    run(40, lags)
    advance(1, 40)
    eigen_chunks(3, 6)
    eigen_end()
    for to in range(41, 53):
        advance_all(to, lags)
    factor_outputs()
    for to in range(53, 40 + 23):
        advance_all(to, lags)
    eigen_pass()

    pltpu.make_async_copy(basis_out.at[z], bout, lsem.at[6]).wait()
    def w_copy(q):
        return rc(wb.at[q], wb.at[q], w_ss.at[q], w_rs.at[q], core)

    home = (z % 2) == xl
    dy = (z // 2 - y + NY) % NY
    shard = jnp.where(dy == 3, 2, jnp.where(dy == 2, 3, dy))

    def mine_first(idx):
        return jnp.where(shard == 2, 1 - idx % 2, idx % 2) == c

    @pl.loop(0, 4)
    def _(idx):
        q = feature_block(shard, idx)

        @pl.when(mine_first(idx))
        def _():
            for h in range(2):
                @pl.when(jnp.logical_not(home))
                def _():
                    rc(xst.at[q, h], xr.at[xh, q, h], xs_ss.at[0, q, h], xs_rs.at[xh, q, h], far).wait_recv()

                rc(xst.at[q, h], xr.at[1 - xh, q, h], xs_ss.at[0, q, h], xs_rs.at[1 - xh, q, h], far).wait_recv()
                wb[q, :, h * HALF : (h + 1) * HALF] = (
                    xr[0, q, h].astype(F32) + xr[1, q, h].astype(F32)
                ).astype(BF)
            w_copy(q).start()

    @pl.loop(0, 4)
    def _(idx):
        q = feature_block(shard, idx)

        @pl.when(jnp.logical_not(mine_first(idx)))
        def _():
            w_copy(q).wait_recv()

        rows = pl.ds(pl.multiple_of(q * PIECE, PIECE), PIECE)
        right[rows, :] = ndot(wb[q], basis_in[...]).astype(BF)

    @pl.when(c == 0)
    def _():
        rc(eigb.at[1], eigb.at[1], ec_ss, ec_rs, core).wait_recv()

    @pl.when(c == 1)
    def _():
        rc(eigb.at[0], eigb.at[0], ec_ss, ec_rs, core).wait_recv()

    ei = eigb[0, 0:1, :]
    for a in range(4):
        rows = slice(a * PIECE, (a + 1) * PIECE)
        eo = jnp.transpose(jnp.broadcast_to(eigb[1, 0:1, rows], (PIECE, PIECE)))
        eo = jnp.concatenate([eo] * 4, axis=1)
        scaled[rows, :] = (tdot(bout[:, rows], right[...]) / (eo * ei + DAMPING)).astype(BF)
    mine = pl.ds(pl.multiple_of((xh * 2 + c) * PIECE, PIECE), PIECE)
    upper = ndot(bout[mine, :], scaled[...]).astype(BF)
    precond[...] = lax.dot_general(
        upper, basis_in[...], (((1,), (1,)), ((), ())), preferred_element_type=F32
    ).astype(BF)

    for k in range(4):
        send_p(k).wait_send()
        send_m(k).wait_send()
    for k in range(2):
        fwd_p(k).wait_send()
        fwd_m(k).wait_send()
        send_x(k).wait_send()

    @pl.loop(0, NU)
    def _(i):
        core_copy(i).wait_send()

        @pl.when(dist(i) != 0)
        def _():
            z_copy(i, zp, ra, a_rs).wait_send()

    rc(ts, tr, tx_ss.at[0], tx_rs.at[0], far).wait_send()
    for k in range(7):
        t_copy(z, k, zp).wait_send()
    for o in range(NF):
        t_core(o).wait_send()

    @pl.when(home)
    def _():
        @pl.loop(0, 4)
        def _(idx):
            q = feature_block(shard, idx)

            @pl.when(mine_first(idx))
            def _():
                for k in range(3):
                    for h in range(2):
                        rc(
                            xst.at[q, h], xr.at[xh, q, h], xs_ss.at[k, q, h], xs_rs.at[xh, q, h], far
                        ).wait_send()

    @pl.loop(0, 4)
    def _(idx):
        @pl.when(mine_first(idx))
        def _():
            w_copy(feature_block(shard, idx)).wait_send()

    rc(eigb.at[0], eigb.at[0], ec_ss, ec_rs, core).wait_send()

    @pl.when((c == 1) & (w == z))
    def _():
        for k in range(1, 8):
            rc(eigb.at[1], eigb.at[1], e_ss.at[k - 1], e_rs, (r, (w + k) % 8)).wait_send()

    for f in range(2):
        for o in range(NF):
            total_copy(f, o).wait()


def update(precond, totals, act_factor, grad_factor, precond_out, act_new, grad_new):
    precond_out[...] = precond[...]
    act_new[0] = DECAY_RATE * act_factor[0] + (1.0 - DECAY_RATE) * totals[0].astype(F32)
    grad_new[0] = DECAY_RATE * grad_factor[0] + (1.0 - DECAY_RATE) * totals[1].astype(F32)


def per_device(acts, cotan, block_ids, basis_in, basis_out, act_factor, grad_factor):
    vm = pltpu.VMEM
    dma = pltpu.SemaphoreType.DMA
    unit = (PIECE, HALF)
    any_spec = pl.BlockSpec(memory_space=pltpu.HBM)
    precond, totals = pl.pallas_call(
        kernel,
        name="kfac",
        out_shape=(
            jax.ShapeDtypeStruct((PIECE, FB), BF),
            jax.ShapeDtypeStruct((2, FB, FB), BF),
        ),
        in_specs=[
            pl.BlockSpec(memory_space=pltpu.SMEM),
            any_spec,
            any_spec,
            pl.BlockSpec(memory_space=pltpu.VMEM),
            any_spec,
            any_spec,
            any_spec,
        ],
        out_specs=(pl.BlockSpec(memory_space=pltpu.VMEM),) * 2,
        scratch_shapes=[
            vm((8, 1024, HALF), BF),
            vm((2, 2, 1024, HALF), BF),
            vm((2, 2 * BLK, FB), BF),
            vm((NU,) + unit, F32),
            vm((NU,) + unit, BF),
            vm((NU,) + unit, BF),
            vm((NU,) + unit, BF),
            vm((NU,) + unit, BF),
            vm((NU,) + unit, BF),
            vm((NU,) + unit, BF),
            vm((NU,) + unit, BF),
            vm((2, 4, 2) + unit, BF),
            vm((4, 2) + unit, BF),
            vm((4, PIECE, FB), BF),
            vm(unit, BF),
            vm(unit, BF),
            vm((2, NF) + unit, BF),
            vm((FB, FB), F32),
            vm((FB, FB), BF),
            vm((FB, FB), BF),
            vm((2, 8, FB), F32),
            vm((8, FB), F32),
            vm((FB, FB), BF),
            vm((FB, FB), BF),
            dma((26,)),
            dma((12,)),
            dma((16,)),
            dma((2,)),
            dma((2,)),
            dma((NU,)),
            dma((NU,)),
            dma((NU,)),
            dma((NU,)),
            dma((NU,)),
            dma((NU,)),
            dma((NU,)),
            dma((3, 4, 2)),
            dma((2, 4, 2)),
            dma((4,)),
            dma((4,)),
            dma((7,)),
            dma((NF,)),
            dma((1,)),
            dma((1,)),
            dma((NF,)),
            dma((NF,)),
            dma((7,)),
            dma,
            dma,
            dma,
        ],
        compiler_params=pltpu.CompilerParams(
            collective_id=0, has_side_effects=True, vmem_limit_bytes=60 << 20
        ),
    )(
        block_ids,
        acts,
        cotan,
        basis_in.reshape(FB, FB),
        basis_out,
        act_factor.reshape(FB, FB),
        grad_factor.reshape(FB, FB),
    )
    steps = 2
    rows = pl.BlockSpec((PIECE // steps, FB), lambda i: (i, 0))
    both = pl.BlockSpec((2, FB // steps, FB), lambda i: (0, i, 0))
    factor = pl.BlockSpec((1, FB // steps, FB), lambda i: (0, i, 0))
    return pl.pallas_call(
        update,
        name="update",
        grid=(steps,),
        in_specs=[rows, both, factor, factor],
        out_specs=(rows, factor, factor),
        out_shape=(
            jax.ShapeDtypeStruct((PIECE, FB), BF),
            jax.ShapeDtypeStruct((1, FB, FB), F32),
            jax.ShapeDtypeStruct((1, FB, FB), F32),
        ),
        compiler_params=pltpu.CompilerParams(vmem_limit_bytes=60 << 20),
    )(precond, totals, act_factor, grad_factor)


def solution(mesh):
    return jax.shard_map(
        per_device,
        mesh=mesh,
        in_specs=(
            P("dp", "worker"),
            P("dp", "worker"),
            P("dp"),
            P("worker", None, None),
            P(),
            P("worker", None, None),
            P("worker", None, None),
        ),
        out_specs=(P("dp", "worker"), P("worker", None, None), P("worker", None, None)),
        check_vma=False,
    )
```

```python
import jax
import jax.numpy as jnp
from jax import lax
from jax.experimental import pallas as pl
from jax.experimental.pallas import tpu as pltpu
from jax.sharding import PartitionSpec as P

MESH = pl.DeviceIdType.MESH
DECAY_RATE = 0.75
DAMPING = 0.03
BLK = 128
NX, NY, NZ = 4, 4, 8
FB = 512
PIECE = 128
HALF = 256
NF = 8
NU = 40
SKIP_FROM = 36
BF = jnp.bfloat16
F32 = jnp.float32


def tdot(a, b):
    return lax.dot_general(a, b, (((0,), (0,)), ((), ())), preferred_element_type=F32)


def ndot(a, b):
    return lax.dot_general(a, b, (((1,), (0,)), ((), ())), preferred_element_type=F32)


def device(x, y, z, c):
    return (z * 4 + (x // 2) * 2 + c, y * 2 + x % 2)


def weight_units():
    units = [(m, 0, h) for m in range(4) for h in range(2)]
    units += [(m, 1, 0) for m in range(4)]
    for m in (4, 5):
        units += [(m, 0, 0), (m, 0, 1), (m, 1, 0)]
    units += [(m, 1, 1) for m in range(6)]
    return units + [(m, e, h) for m in (6, 7) for e in range(2) for h in range(2)]


def packed(values, bits):
    word = sum(v << (bits * k) for k, v in enumerate(values))
    return word - (1 << 32) if word >= 1 << 31 else word


def field(word, place, bits):
    return lax.shift_right_logical(word, jnp.int32(bits) * place) & ((1 << bits) - 1)


PAIR_ACTS = [packed([2 * m + e for m, e, _ in weight_units()[g : g + 8]], 4) for g in range(0, 32, 8)]
PART = packed([h for _, _, h in weight_units()], 1)


def shard_offset(m, c):
    side = 1 - c if m in (3, 7) else c
    return 0 if m < 2 else 2 if m in (4, 6) else 3 if side else 1


OFFSETS = [
    [packed([shard_offset(m, c) for m, _, _ in weight_units()[g : g + 16]], 2) for g in (0, 16)] for c in range(2)
]


def unit_parts(i):
    j = i - NF
    group = j >> 3
    word = jnp.int32(PAIR_ACTS[0])
    for g in range(1, 4):
        word = jnp.where(group == g, jnp.int32(PAIR_ACTS[g]), word)
    both = field(word, j & 7, 4)
    return both >> 1, both & 1, field(jnp.int32(PART), j, 1)


def kept_piece(m, c):
    return 2 * m + jnp.where((m == 3) | (m == 7), 1 - c, c)


def piece_source(n):
    m = n // 2
    far = (m == 4) | (m == 6)
    k = jnp.where(m < 2, 0, jnp.where(far, 3, 1 + n % 2))
    far_idx = jnp.where(m == 6, 2, 0) + n % 2
    idx = jnp.where(m < 2, n, jnp.where(far, far_idx, jnp.where(m < 4, m - 2, (m - 1) // 2)))
    return k, idx


def feature_block(k, idx):
    return jnp.where(k == 3, (idx % 2) * 2 + idx // 2, jnp.where(k == 1, (idx + 2) % 4, idx))


def y_offset(k):
    return jnp.where(k == 2, 3, jnp.where(k == 3, 2, k))


def kernel(
    ids, acts, cotan, basis_in, basis_out, act_factor, grad_factor,
    precond, totals,
    cotb, actb, smp, own, cout, cin, zout, ra, rb, rcc, rd, xr, xst, wb, ts, tr, tb, fac, ebas, bout, eigb, eigs, scaled, right,
    lsem, y_ss, y_rs, x_ss, x_rs, c_ss, c_rs, z_ss, a_rs, b_rs, cc_rs, d_rs, xs_ss, xs_rs, w_ss, w_rs, t_ss, t_rs, tx_ss, tx_rs,
    tc_ss, tc_rs, e_ss, e_rs, ec_ss, ec_rs,
):
    r = lax.axis_index("dp")
    w = lax.axis_index("worker")
    z, xh, c = r // 4, (r // 2) % 2, r % 2
    y, xl = w // 2, w % 2
    x = xh * 2 + xl
    oc = 1 - c

    def at(dx=0, dy=0, dz=0):
        return device((x + dx) % NX, (y + dy) % NY, (z + dz) % NZ, c)

    core = device(x, y, z, oc)
    zp, zm, zp2, zm2 = at(dz=1), at(dz=7), at(dz=2), at(dz=6)
    yp, ym = at(dy=1), at(dy=3)
    far_x = (1 - xh) * 2 + xl
    part_x = xh * 2 + (1 - xl)
    cross_x = (1 - xh) * 2 + (1 - xl)
    partner = device(part_x, y, z, c)
    far = device(far_x, y, z, c)
    cross = device(cross_x, y, z, c)

    def rc(src, dst, ss, rs, dev):
        return pltpu.make_async_remote_copy(
            src_ref=src, dst_ref=dst, send_sem=ss, recv_sem=rs, device_id=dev, device_id_type=MESH
        )

    loads = []
    for q in range(4):
        into = cotb.at[q // 2, :, pl.ds((q % 2) * PIECE, PIECE)]
        loads.append(pltpu.make_async_copy(cotan.at[:, pl.ds(q * PIECE, PIECE)], into, lsem.at[q]))
    for h in range(2):
        loads.append(pltpu.make_async_copy(acts.at[:, pl.ds(h * HALF, HALF)], actb.at[xl, h], lsem.at[4 + h]))
    loads.append(pltpu.make_async_copy(basis_out.at[z], bout, lsem.at[6]))
    for cp in loads:
        cp.start()

    @pl.when(c == 0)
    def _():
        pltpu.make_async_copy(basis_in, ebas, lsem.at[7]).start()
        pltpu.make_async_copy(act_factor, fac, lsem.at[8]).start()

    @pl.when(c == 1)
    def _():
        pltpu.make_async_copy(basis_out.at[w], ebas, lsem.at[7]).start()
        pltpu.make_async_copy(grad_factor, fac, lsem.at[8]).start()

    barrier = pltpu.get_barrier_semaphore()
    for k in range(1, 8):
        wk = (w + k) % 8
        pl.semaphore_signal(barrier, inc=1, device_id=(r, wk), device_id_type=MESH)
    for dev in (core, zp, zm, zp2, zm2, far, cross):
        pl.semaphore_signal(barrier, inc=1, device_id=dev, device_id_type=MESH)
    pl.semaphore_wait(barrier, 14)

    def piece(n):
        return cotb.at[n // 2, :, pl.ds((n % 2) * PIECE, PIECE)]

    def send_p(k):
        n = (5, 7, 11, 15)[k]
        return rc(cotan.at[:, pl.ds(k * PIECE, PIECE)], piece(n), y_ss.at[k], y_rs.at[n], yp)

    def send_m(k):
        n = (4, 6, 10, 14)[k]
        q = (k + 2) % 4
        return rc(cotan.at[:, pl.ds(q * PIECE, PIECE)], piece(n), y_ss.at[4 + k], y_rs.at[n], ym)

    def fwd_p(k):
        src, dst = (5, 7)[k], (8, 12)[k]
        return rc(piece(src), piece(dst), y_ss.at[8 + k], y_rs.at[dst], yp)

    def fwd_m(k):
        src, dst = (4, 6)[k], (9, 13)[k]
        return rc(piece(src), piece(dst), y_ss.at[10 + k], y_rs.at[dst], ym)

    def send_x(h):
        return rc(acts.at[:, pl.ds(h * HALF, HALF)], actb.at[xl, h], x_ss.at[h], x_rs.at[h], partner)

    def recv_x(h):
        return rc(acts.at[:, pl.ds(h * HALF, HALF)], actb.at[1 - xl, h], x_ss.at[h], x_rs.at[h], partner)

    for k in range(2):
        send_p(k).start()
        send_m(k).start()
        send_x(k).start()

    def wait_piece(n):
        rc(piece(n), piece(n), y_ss.at[0], y_rs.at[n], yp).wait_recv()

    for cp in loads[:6]:
        cp.wait()

    offsets = [jnp.where(c == 0, jnp.int32(OFFSETS[0][g]), jnp.int32(OFFSETS[1][g])) for g in range(2)]

    def dist(i):
        j = i - NF
        dy = field(jnp.where(j < 16, offsets[0], offsets[1]), j & 15, 2)
        to = jnp.where(i < NF, i, 2 * ((y + dy) & (NY - 1)) + xl)
        return (to - z + NZ) & (NZ - 1)

    def along(i, steps):
        return at(dz=jnp.where(i % 2 == 0, steps, NZ - steps))

    def core_copy(i):
        return rc(cout.at[i], cin.at[i], c_ss.at[i], c_rs.at[i], core)

    def z_copy(i, dev, land, sem):
        return rc(zout.at[i], land.at[i], z_ss.at[i], sem.at[i], dev)

    lands = {"a": (ra, a_rs), "b": (rb, b_rs), "c": (rcc, cc_rs), "d": (rd, d_rs)}

    def send_z(i, steps, slot):
        z_copy(i, along(i, steps), *lands[slot]).start()

    def recv_z(i, slots):
        for slot in slots:
            z_copy(i, zp, *lands[slot]).wait_recv()
        acc = own[i]
        for slot in slots:
            acc = acc + lands[slot][0][i].astype(F32)
        return acc.astype(BF)

    def compute_factor():
        scale_own = jnp.where(c == 0, 1.0 / 8192, 4.0).astype(F32)
        scale_other = jnp.where(c == 0, 4.0, 1.0 / 8192).astype(F32)
        for s in range(2):
            into = slice(s * BLK, (s + 1) * BLK)
            for h in range(2):
                block = actb[xl, h, :BLK, :]
                for k in range(1, 8):
                    block = jnp.where(ids[s] == k, actb[xl, h, k * BLK : (k + 1) * BLK, :], block)
                smp[0, into, h * HALF : (h + 1) * HALF] = block
            for q in range(4):
                cols = slice((q % 2) * PIECE, (q % 2 + 1) * PIECE)
                block = cotb[q // 2, :BLK, cols]
                for k in range(1, 8):
                    block = jnp.where(ids[s] == k, cotb[q // 2, k * BLK : (k + 1) * BLK, cols], block)
                smp[1, into, q * PIECE : (q + 1) * PIECE] = block

        @pl.loop(0, NF)
        def _(i):
            left = pl.ds(pl.multiple_of((i // 2) * PIECE, PIECE), PIECE)
            cols = pl.ds(pl.multiple_of((i % 2) * HALF, HALF), HALF)
            cout[i] = (tdot(smp[oc, :, left], smp[oc, :, cols]) * scale_other).astype(BF)
            core_copy(i).start()
            own[i] = tdot(smp[c, :, left], smp[c, :, cols]) * scale_own

    def compute(i):
        m, e, h = unit_parts(i)
        ea = jnp.where(e == 0, xl, 1 - xl)
        both = tdot(cotb[m], actb[ea, h])
        lower = kept_piece(m, c) % 2 == 0
        cout[i] = jnp.where(lower, both[PIECE:], both[:PIECE]).astype(BF)
        core_copy(i).start()
        own[i] = jnp.where(lower, both[:PIECE], both[PIECE:])

    def way(i):
        d = dist(i)
        return jnp.where(i % 2 == 0, d, (NZ - d) % NZ), i < NF, (i >= NF) & (i < SKIP_FROM), i >= SKIP_FROM

    def merge(i):
        core_copy(i).wait_recv()
        acc = own[i] + cin[i].astype(F32)
        own[i] = acc
        d, tree, chain, skip = way(i)
        near_up = (tree & ((d == 1) | (d == 3))) | (skip & (d == 3))
        near_down = tree & (d == 7)

        @pl.when((d == 4) | (d == 5) | near_up | near_down)
        def _():
            zout[i] = acc.astype(BF)

        @pl.when((d == 4) & tree)
        def _():
            send_z(i, 2, "a")

        @pl.when((d == 4) & skip)
        def _():
            send_z(i, 2, "c")

        @pl.when(((d == 4) & chain) | (tree & (d == 1)) | (skip & (d == 3)))
        def _():
            send_z(i, 1, "a")

        @pl.when(tree & (d == 3))
        def _():
            send_z(i, 1, "b")

        @pl.when((d == 5) | near_down)
        def _():
            send_z(i, 7, "b")

    def pass_on(i, cond, slots, steps, slot):
        @pl.when(cond)
        def _():
            zout[i] = recv_z(i, slots)
            send_z(i, steps, slot)

    def finish_z(i, cond, slots):
        @pl.when(cond)
        def _():
            total = recv_z(i, slots)

            @pl.when(i < NF)
            def _():
                ts[...] = total
                rc(ts, tr, tx_ss.at[0], tx_rs.at[0], far).start()

            @pl.when(i >= NF)
            def _():
                m, e, h = unit_parts(i)
                q = feature_block(*piece_source(kept_piece(m, c)))

                @pl.when(e == 0)
                def _():
                    xr[xh, q, h] = total
                    rc(xr.at[xh, q, h], xr.at[xh, q, h], xs_ss.at[0, q, h], xs_rs.at[xh, q, h], far).start()

                @pl.when(e == 1)
                def _():
                    xst[q, h] = total
                    rc(xst.at[q, h], xr.at[xh, q, h], xs_ss.at[1, q, h], xs_rs.at[xh, q, h], partner).start()
                    rc(xst.at[q, h], xr.at[xh, q, h], xs_ss.at[2, q, h], xs_rs.at[xh, q, h], cross).start()

    def hop_1(i):
        d, tree, chain, skip = way(i)
        pass_on(i, (d == 3) & chain, "a", 1, "a")
        pass_on(i, (d == 2) & skip, "ac", 1, "a")
        pass_on(i, (d == 6) & (chain | skip), "b", 7, "b")
        pass_on(i, (d == 2) & tree, "ab", 2, "c")
        pass_on(i, (d == 6) & tree, "b", 6, "d")

    def hop_2(i):
        d, tree, chain, skip = way(i)
        pass_on(i, ((d == 2) & chain) | ((d == 1) & skip), "a", 1, "a")
        pass_on(i, (d == 7) & (chain | skip), "b", 7, "b")
        finish_z(i, (d == 0) & tree, "abcd")

    def hop_3(i):
        d, _, chain, skip = way(i)
        pass_on(i, (d == 1) & chain, "a", 1, "a")
        finish_z(i, (d == 0) & skip, "ab")

    def hop_4(i):
        d, _, chain, _ = way(i)
        finish_z(i, (d == 0) & chain, "ab")

    stages = (compute, merge, hop_1, hop_2, hop_3, hop_4)
    done = [NF] * len(stages)

    def advance(stage, to):
        lo, to = done[stage], min(to, NU)
        if to > lo:
            pl.loop(lo, to)(stages[stage])
            done[stage] = to

    def advance_all(to, lags):
        for stage in range(len(stages) - 1, 0, -1):
            advance(stage, to - lags[stage])

    def run(to, lags):
        lo = done[0]
        advance_all(lo, lags)

        @pl.loop(lo, to)
        def _(i):
            compute(i)
            for stage in range(1, len(stages)):
                first, lag = done[stage], lags[stage]
                if to - lag > first:
                    if lo - lag >= first:
                        stages[stage](i - lag)
                    else:
                        pl.when(i - lag >= first)(lambda stage=stage, lag=lag: stages[stage](i - lag))

        done[0] = to
        for stage in range(1, len(stages)):
            done[stage] = max(done[stage], to - lags[stage])

    def each_factor(step):
        pl.loop(0, NF)(step)

    def t_copy(o, k, dev):
        return rc(tb.at[c, o], tb.at[c, o], t_ss.at[k], t_rs.at[o], dev)

    def t_core(o):
        return rc(tb.at[c, o], tb.at[c, o], tc_ss.at[o], tc_rs.at[o], core)

    def t_core_recv(o):
        return rc(tb.at[oc, o], tb.at[oc, o], tc_ss.at[o], tc_rs.at[o], core)

    def origin(dz):
        return (z + dz) % NZ

    def spread_1():
        rc(ts, tr, tx_ss.at[0], tx_rs.at[0], far).wait_recv()
        tb[c, z] = (ts[...].astype(F32) + tr[...].astype(F32)).astype(BF)
        for k, dev in enumerate((zp, zm, zp2, zm2)):
            t_copy(z, k, dev).start()
        t_core(z).start()

    def t_arrived(dz):
        o = origin(dz)
        t_copy(o, 0, zp).wait_recv()
        t_core(o).start()

    def spread_2():
        back, ahead = jnp.where(c == 0, 6, 2), jnp.where(c == 0, 2, 6)
        t_arrived(back)
        t_copy(origin(back), 4, along(c, 1)).start()
        t_copy(origin(back), 5, along(c, 2)).start()
        t_arrived(ahead)
        t_copy(origin(ahead), 6, along(c, 7)).start()
        t_arrived(7)
        t_arrived(1)

    def spread_3():
        t_arrived(5)
        t_arrived(3)
        t_arrived(4)

    def eigen_chunks(lo, hi):
        if lo == 6:
            pltpu.make_async_copy(act_factor, fac, lsem.at[8]).wait()
            pltpu.make_async_copy(basis_in, ebas, lsem.at[7]).wait()
            eigs[...] = jnp.zeros_like(eigs)

        @pl.loop(lo, hi)
        def _(dz):
            o = (z + dz) % NZ
            rows = pl.ds(pl.multiple_of((o // 2) * PIECE, PIECE), PIECE)
            cols = pl.ds(pl.multiple_of((o % 2) * HALF, HALF), HALF)
            new = DECAY_RATE * fac[rows, cols] + (1.0 - DECAY_RATE) * tb[c, o].astype(F32)
            basis = ebas[cols, :]
            prod = jnp.zeros((PIECE, FB), F32)
            for _ in range(3):
                part = new.astype(BF)
                prod = prod + ndot(part, basis)
                new = new - part.astype(F32)
            prod = prod * ebas[rows, :].astype(F32)
            eigs[...] += jnp.sum(prod.reshape(PIECE // 8, 8, FB), axis=0)

    def total_copy(f, o):
        into = totals.at[f, pl.ds((o // 2) * PIECE, PIECE), pl.ds((o % 2) * HALF, HALF)]
        return pltpu.make_async_copy(tb.at[f, o], into, lsem.at[10 + f * NF + o])

    def factor_outputs():
        for o in range(NF):
            t_core_recv(o).wait_recv()
        for f in range(2):
            for o in range(NF):
                total_copy(f, o).start()

    def eigen_end():
        eig = jnp.broadcast_to(jnp.sum(eigs[...], axis=0, keepdims=True), (8, FB))

        @pl.when(c == 0)
        def _():
            eigb[0] = eig
            rc(eigb.at[0], eigb.at[0], ec_ss, ec_rs, core).start()

        @pl.when((c == 1) & (w == z))
        def _():
            eigb[1] = eig
            for k in range(1, 8):
                rc(eigb.at[1], eigb.at[1], e_ss.at[k - 1], e_rs, (r, (w + k) % 8)).start()

    def eigen_pass():
        @pl.when(c == 1)
        def _():
            @pl.when(w != z)
            def _():
                rc(eigb.at[1], eigb.at[1], e_ss.at[0], e_rs, (r, z)).wait_recv()

            rc(eigb.at[1], eigb.at[1], ec_ss, ec_rs, core).start()

    lags = (0, 2, 7, 12, 17, 22)
    compute_factor()
    each_factor(merge)
    run(12, lags)
    advance(1, 12)
    each_factor(hop_1)
    wait_piece(5)
    fwd_p(0).start()
    send_p(2).start()
    wait_piece(4)
    fwd_m(0).start()
    send_m(2).start()
    run(14, lags)
    advance(1, 14)
    advance(2, 12)
    each_factor(hop_2)
    wait_piece(7)
    fwd_p(1).start()
    send_p(3).start()
    wait_piece(6)
    fwd_m(1).start()
    send_m(3).start()
    run(16, lags)
    recv_x(0).wait_recv()
    run(20, lags)
    advance(1, 20)
    advance(3, 12)
    advance(2, 14)
    spread_1()
    wait_piece(8)
    wait_piece(9)
    run(23, lags)
    advance(1, 23)
    advance(4, 12)
    advance(3, 14)
    advance(2, 20)
    spread_2()
    eigen_chunks(6, 11)
    wait_piece(10)
    wait_piece(11)
    run(26, lags)
    recv_x(1).wait_recv()
    run(32, lags)
    spread_3()
    wait_piece(12)
    wait_piece(13)
    run(36, lags)
    wait_piece(14)
    wait_piece(15)
    run(40, lags)
    advance(1, 40)
    eigen_chunks(3, 6)
    eigen_end()
    for to in range(41, 53):
        advance_all(to, lags)
    factor_outputs()
    for to in range(53, 40 + 23):
        advance_all(to, lags)
    eigen_pass()

    for k in range(4):
        send_p(k).wait_send()
        send_m(k).wait_send()
    for k in range(2):
        fwd_p(k).wait_send()
        fwd_m(k).wait_send()
        send_x(k).wait_send()

    @pl.loop(0, NU)
    def _(i):
        core_copy(i).wait_send()

        @pl.when(dist(i) != 0)
        def _():
            z_copy(i, zp, ra, a_rs).wait_send()

    rc(ts, tr, tx_ss.at[0], tx_rs.at[0], far).wait_send()
    for k in range(7):
        t_copy(z, k, zp).wait_send()
    for o in range(NF):
        t_core(o).wait_send()

    pltpu.make_async_copy(basis_out.at[z], bout, lsem.at[6]).wait()
    def w_copy(q):
        return rc(wb.at[q], wb.at[q], w_ss.at[q], w_rs.at[q], core)

    home = (z % 2) == xl
    dy = (z // 2 - y + NY) % NY
    shard = jnp.where(dy == 3, 2, jnp.where(dy == 2, 3, dy))

    def mine_first(idx):
        return jnp.where(shard == 2, 1 - idx % 2, idx % 2) == c

    @pl.loop(0, 4)
    def _(idx):
        q = feature_block(shard, idx)

        @pl.when(mine_first(idx))
        def _():
            for h in range(2):
                @pl.when(jnp.logical_not(home))
                def _():
                    rc(xst.at[q, h], xr.at[xh, q, h], xs_ss.at[0, q, h], xs_rs.at[xh, q, h], far).wait_recv()

                rc(xst.at[q, h], xr.at[1 - xh, q, h], xs_ss.at[0, q, h], xs_rs.at[1 - xh, q, h], far).wait_recv()
                wb[q, :, h * HALF : (h + 1) * HALF] = (
                    xr[0, q, h].astype(F32) + xr[1, q, h].astype(F32)
                ).astype(BF)
            w_copy(q).start()

    @pl.loop(0, 4)
    def _(idx):
        q = feature_block(shard, idx)

        @pl.when(jnp.logical_not(mine_first(idx)))
        def _():
            w_copy(q).wait_recv()

        rows = pl.ds(pl.multiple_of(q * PIECE, PIECE), PIECE)
        right[rows, :] = ndot(wb[q], basis_in[...]).astype(BF)

    @pl.when(c == 0)
    def _():
        rc(eigb.at[1], eigb.at[1], ec_ss, ec_rs, core).wait_recv()

    @pl.when(c == 1)
    def _():
        rc(eigb.at[0], eigb.at[0], ec_ss, ec_rs, core).wait_recv()

    ei = eigb[0, 0:1, :]
    for a in range(4):
        rows = slice(a * PIECE, (a + 1) * PIECE)
        eo = jnp.transpose(jnp.broadcast_to(eigb[1, 0:1, rows], (PIECE, PIECE)))
        eo = jnp.concatenate([eo] * 4, axis=1)
        scaled[rows, :] = (tdot(bout[:, rows], right[...]) / (eo * ei + DAMPING)).astype(BF)
    mine = pl.ds(pl.multiple_of((xh * 2 + c) * PIECE, PIECE), PIECE)
    upper = ndot(bout[mine, :], scaled[...]).astype(BF)
    precond[...] = lax.dot_general(
        upper, basis_in[...], (((1,), (1,)), ((), ())), preferred_element_type=F32
    ).astype(BF)

    @pl.when(home)
    def _():
        @pl.loop(0, 4)
        def _(idx):
            q = feature_block(shard, idx)

            @pl.when(mine_first(idx))
            def _():
                for k in range(3):
                    for h in range(2):
                        rc(
                            xst.at[q, h], xr.at[xh, q, h], xs_ss.at[k, q, h], xs_rs.at[xh, q, h], far
                        ).wait_send()

    @pl.loop(0, 4)
    def _(idx):
        @pl.when(mine_first(idx))
        def _():
            w_copy(feature_block(shard, idx)).wait_send()

    rc(eigb.at[0], eigb.at[0], ec_ss, ec_rs, core).wait_send()

    @pl.when((c == 1) & (w == z))
    def _():
        for k in range(1, 8):
            rc(eigb.at[1], eigb.at[1], e_ss.at[k - 1], e_rs, (r, (w + k) % 8)).wait_send()

    for f in range(2):
        for o in range(NF):
            total_copy(f, o).wait()


def update(precond, totals, act_factor, grad_factor, precond_out, act_new, grad_new):
    precond_out[...] = precond[...]
    act_new[0] = DECAY_RATE * act_factor[0] + (1.0 - DECAY_RATE) * totals[0].astype(F32)
    grad_new[0] = DECAY_RATE * grad_factor[0] + (1.0 - DECAY_RATE) * totals[1].astype(F32)


def per_device(acts, cotan, block_ids, basis_in, basis_out, act_factor, grad_factor):
    vm = pltpu.VMEM
    dma = pltpu.SemaphoreType.DMA
    unit = (PIECE, HALF)
    any_spec = pl.BlockSpec(memory_space=pltpu.HBM)
    precond, totals = pl.pallas_call(
        kernel,
        name="kfac",
        out_shape=(
            jax.ShapeDtypeStruct((PIECE, FB), BF),
            jax.ShapeDtypeStruct((2, FB, FB), BF),
        ),
        in_specs=[
            pl.BlockSpec(memory_space=pltpu.SMEM),
            any_spec,
            any_spec,
            pl.BlockSpec(memory_space=pltpu.VMEM),
            any_spec,
            any_spec,
            any_spec,
        ],
        out_specs=(pl.BlockSpec(memory_space=pltpu.VMEM),) * 2,
        scratch_shapes=[
            vm((8, 1024, HALF), BF),
            vm((2, 2, 1024, HALF), BF),
            vm((2, 2 * BLK, FB), BF),
            vm((NU,) + unit, F32),
            vm((NU,) + unit, BF),
            vm((NU,) + unit, BF),
            vm((NU,) + unit, BF),
            vm((NU,) + unit, BF),
            vm((NU,) + unit, BF),
            vm((NU,) + unit, BF),
            vm((NU,) + unit, BF),
            vm((2, 4, 2) + unit, BF),
            vm((4, 2) + unit, BF),
            vm((4, PIECE, FB), BF),
            vm(unit, BF),
            vm(unit, BF),
            vm((2, NF) + unit, BF),
            vm((FB, FB), F32),
            vm((FB, FB), BF),
            vm((FB, FB), BF),
            vm((2, 8, FB), F32),
            vm((8, FB), F32),
            vm((FB, FB), BF),
            vm((FB, FB), BF),
            dma((26,)),
            dma((12,)),
            dma((16,)),
            dma((2,)),
            dma((2,)),
            dma((NU,)),
            dma((NU,)),
            dma((NU,)),
            dma((NU,)),
            dma((NU,)),
            dma((NU,)),
            dma((NU,)),
            dma((3, 4, 2)),
            dma((2, 4, 2)),
            dma((4,)),
            dma((4,)),
            dma((7,)),
            dma((NF,)),
            dma((1,)),
            dma((1,)),
            dma((NF,)),
            dma((NF,)),
            dma((7,)),
            dma,
            dma,
            dma,
        ],
        compiler_params=pltpu.CompilerParams(
            collective_id=0, has_side_effects=True, vmem_limit_bytes=60 << 20
        ),
    )(
        block_ids,
        acts,
        cotan,
        basis_in.reshape(FB, FB),
        basis_out,
        act_factor.reshape(FB, FB),
        grad_factor.reshape(FB, FB),
    )
    steps = 2
    rows = pl.BlockSpec((PIECE // steps, FB), lambda i: (i, 0))
    both = pl.BlockSpec((2, FB // steps, FB), lambda i: (0, i, 0))
    factor = pl.BlockSpec((1, FB // steps, FB), lambda i: (0, i, 0))
    return pl.pallas_call(
        update,
        name="update",
        grid=(steps,),
        in_specs=[rows, both, factor, factor],
        out_specs=(rows, factor, factor),
        out_shape=(
            jax.ShapeDtypeStruct((PIECE, FB), BF),
            jax.ShapeDtypeStruct((1, FB, FB), F32),
            jax.ShapeDtypeStruct((1, FB, FB), F32),
        ),
        compiler_params=pltpu.CompilerParams(vmem_limit_bytes=60 << 20),
    )(precond, totals, act_factor, grad_factor)


def solution(mesh):
    return jax.shard_map(
        per_device,
        mesh=mesh,
        in_specs=(
            P("dp", "worker"),
            P("dp", "worker"),
            P("dp"),
            P("worker", None, None),
            P(),
            P("worker", None, None),
            P("worker", None, None),
        ),
        out_specs=(P("dp", "worker"), P("worker", None, None), P("worker", None, None)),
        check_vma=False,
    )
```
